128 devices in a mesh: section: 8 (over y, x_hi), seq: 16 (over x_lo, z, core).
Axes of the slice: x: 4 (x_hi: 2, x_lo: 2; x = x_hi * 2 + x_lo), y: 4, z: 4, core: 2. Of those that a mesh axis runs over, the one named last changes fastest.
Arguments:
- teacher_query_array: bfloat16 [8, 4096, 4096], P('section', 'seq'), may hold values from -8 to 8
- teacher_keys: bfloat16 [8, 4096, 512], P('section', 'seq'), may hold values from -8 to 8
- teacher_value_array: bfloat16 [8, 4096, 512], P('section', 'seq'), may hold values from -6 to 6
- projection: bfloat16 [8, 8, 512, 128], P('section'), may hold values from -0.25 to 0.25
- student_query_array: bfloat16 [8, 2048, 2048], P('section', 'seq'), may hold values from -8 to 8
- student_keys: bfloat16 [8, 2048, 512], P('section', 'seq'), may hold values from -8 to 8
- student_value_array: bfloat16 [8, 2048, 512], P('section', 'seq'), may hold values from -6 to 6
Outputs:
- grad_student_q: float32 [8, 2048, 2048], P('section', 'seq')
- grad_student_keys: float32 [8, 2048, 512], P('section', 'seq')
- grad_student_values: float32 [8, 2048, 512], P('section', 'seq')
- per_token_loss: float32 [8, 2048], P('section', 'seq')
The draws below stay inside these ranges and needn't reach their ends.
All inputs are finite; a program needn't handle non-finite values.
Results may differ from the reference program's by a relative error of at most 0.03.
Values may be sent and summed in bfloat16 or wider, within the bound.
A program may use at most 128 MiB of HBM per device.

```python
import math
import jax
import jax.numpy as jnp
from jax import lax

TOK_DEV = 256
HEAD_SIZE = 128
TEACHER_Q_HEADS = 64
TEACHER_KV_HEADS = 8
STUDENT_Q_HEADS = 16
STUDENT_KV_HEADS = 4
LAYER_PAIRS = 4
TOKEN_COUNT = 4096
N_SEQ = 16


def drawn_draw(key, salt_value, tensor_shape):
    drawn = jax.random.normal(jax.random.fold_in(key, salt_value), tensor_shape, dtype=jnp.float32)
    return jnp.clip(drawn, -4.0, 4.0)


def with_positions(key, salt_value, drawn):
    entries, rows, width = drawn.shape
    heads = width // HEAD_SIZE
    pairs = HEAD_SIZE // 8
    half_rows = TOK_DEV // 2
    row_ids = jnp.arange(rows, dtype=jnp.int32)
    entry_ids = jnp.arange(entries, dtype=jnp.int32)
    position = (TOK_DEV * (row_ids // half_rows))[None, :] + (half_rows * (entry_ids % 2))[:, None] + (row_ids % half_rows)[None, :]
    window = TOK_DEV / 8.0
    strength = math.log(4.0 * TOKEN_COUNT / TOK_DEV)
    amplitude = math.sqrt(strength * math.sqrt(HEAD_SIZE) / pairs)
    rates = jax.random.uniform(jax.random.fold_in(key, 9101), (entries // 2, pairs), dtype=jnp.float32, minval=0.05, maxval=1.0) * (math.pi / window)
    rates = jnp.repeat(rates, 2, axis=0)
    phases = position.astype(jnp.float32)[:, :, None] * rates[:, None, :]
    waves = jnp.concatenate([jnp.cos(phases), jnp.sin(phases)], -1)
    wobble = jax.random.uniform(jax.random.fold_in(key, salt_value), (entries, rows, heads, 2 * pairs), dtype=jnp.float32, minval=0.85, maxval=1.15)
    positional = waves[:, :, None, :] * amplitude * wobble
    grid = drawn.reshape(entries, rows, heads, HEAD_SIZE)
    grid = jnp.concatenate([grid[..., :HEAD_SIZE - 2 * pairs], positional], -1)
    return grid.reshape(entries, rows, width)


def draw_teacher_query_array(key, part):
    tensor_shape = (2 * LAYER_PAIRS, TOKEN_COUNT, TEACHER_Q_HEADS // 2 * HEAD_SIZE)
    drawn = drawn_draw(key, 101, tensor_shape)
    return drawn.astype(jnp.bfloat16)


def draw_teacher_keys(key, part):
    tensor_shape = (2 * LAYER_PAIRS, TOKEN_COUNT, TEACHER_KV_HEADS // 2 * HEAD_SIZE)
    drawn = drawn_draw(key, 102, tensor_shape)
    return drawn.astype(jnp.bfloat16)


def draw_student_query_array(key, part):
    tensor_shape = (2 * LAYER_PAIRS, TOKEN_COUNT // 2, STUDENT_Q_HEADS * HEAD_SIZE)
    drawn = with_positions(key, 9201, drawn_draw(key, 103, tensor_shape))
    return drawn.astype(jnp.bfloat16)


def draw_student_keys(key, part):
    tensor_shape = (2 * LAYER_PAIRS, TOKEN_COUNT // 2, STUDENT_KV_HEADS * HEAD_SIZE)
    drawn = with_positions(key, 9202, drawn_draw(key, 104, tensor_shape))
    return drawn.astype(jnp.bfloat16)


def steps_of(own_key, extent, shards, least, high):
    factor_of = 1.0
    for dim, blocks in shards:
        draws = jax.random.uniform(jax.random.fold_in(jax.random.fold_in(own_key, 6), dim), (blocks,), jnp.float32, least / len(shards), high / len(shards))
        factor_of = factor_of * jnp.repeat(jnp.exp(draws), extent[dim] // blocks).reshape((-1,) + (1,) * (len(extent) - 1 - dim))
    return factor_of


def noise(rng, shape, spread, most, split=(), kind=jnp.bfloat16):
    factor_of = steps_of(rng, shape, split, -0.22, 0.18) if split else 1.0
    result = jax.random.normal(rng, shape, jnp.float32) * spread * factor_of
    return jnp.minimum(jnp.maximum(result, -most), most).astype(kind)


def setup_inputs(seed: int = 0) -> dict:
    streams_of = jax.random.split(jax.random.key(seed), 8)
    return {
        "teacher_query_array": draw_teacher_query_array(jax.random.fold_in(streams_of[7], 71), 0),
        "teacher_keys": draw_teacher_keys(jax.random.fold_in(streams_of[7], 71), 0),
        "teacher_value_array": noise(streams_of[2], (2 * LAYER_PAIRS, TOKEN_COUNT, (TEACHER_KV_HEADS // 2) * HEAD_SIZE), 1.0, 6.0, ((0, 8), (1, 16))),
        "projection": noise(streams_of[3], (2 * LAYER_PAIRS, STUDENT_Q_HEADS // 2, (TEACHER_Q_HEADS // STUDENT_Q_HEADS) * HEAD_SIZE, HEAD_SIZE), ((TEACHER_Q_HEADS // STUDENT_Q_HEADS) * HEAD_SIZE) ** -0.5, 0.25, ((0, 8),)),
        "student_query_array": draw_student_query_array(jax.random.fold_in(streams_of[7], 71), 0),
        "student_keys": draw_student_keys(jax.random.fold_in(streams_of[7], 71), 0),
        "student_value_array": noise(streams_of[6], (2 * LAYER_PAIRS, TOKEN_COUNT // 2, STUDENT_KV_HEADS * HEAD_SIZE), 1.0, 6.0, ((0, 8), (1, 16))),
    }


floor_score = -1e+30

def reverted(operand):
    return lax.optimization_barrier(operand.astype(jnp.bfloat16)).astype(jnp.float32)

def causal_scores(queries, key_grid, query_pos, key_pos):
    scores = jnp.einsum('qgjd,kgd->gjqk', queries.astype(jnp.float32), key_grid.astype(jnp.float32)) * (1.0 / math.sqrt(HEAD_SIZE))
    allowed = key_pos[None, None, None, :] <= query_pos[None, None, :, None]
    return (jnp.where(allowed, scores, floor_score), allowed)

def softmax_parts(scores, allowed):
    row_peak = lax.optimization_barrier(jnp.max(scores, axis=-1))
    weights = jnp.where(allowed, jnp.exp(scores - row_peak[..., None]), 0.0)
    row_total = lax.optimization_barrier(jnp.sum(weights, axis=-1))
    return (row_peak, weights, row_total)

def attend(weights, row_total, value_grid):
    mixed = jnp.einsum('gjqk,kgd->qgjd', reverted(weights), value_grid.astype(jnp.float32))
    return mixed / jnp.transpose(row_total, (2, 0, 1))[..., None]

def teacher_context(queries, key_rows, value_rows):
    heads_of_keys = TEACHER_KV_HEADS
    heads_per_group = TEACHER_Q_HEADS // TEACHER_KV_HEADS
    rows_per_block = math.gcd(TOKEN_COUNT, 256)
    key_grid = key_rows.reshape(TOKEN_COUNT, heads_of_keys, HEAD_SIZE)
    value_grid = value_rows.reshape(TOKEN_COUNT, heads_of_keys, HEAD_SIZE)
    key_pos = jnp.arange(TOKEN_COUNT, dtype=jnp.int32)

    def query_block(block_index):
        offset = (block_index * rows_per_block).astype(jnp.int32)
        block_queries = lax.dynamic_slice_in_dim(queries, offset, rows_per_block, 0).reshape(rows_per_block, heads_of_keys, heads_per_group, HEAD_SIZE)
        query_pos = offset + jnp.arange(rows_per_block, dtype=jnp.int32)
        scores, allowed = causal_scores(block_queries, key_grid, query_pos, key_pos)
        row_peak, weights, row_total = softmax_parts(scores, allowed)
        return attend(weights, row_total, value_grid).astype(jnp.bfloat16).reshape(rows_per_block, TEACHER_Q_HEADS * HEAD_SIZE)
    blocks = lax.map(query_block, jnp.arange(TOKEN_COUNT // rows_per_block, dtype=jnp.int32))
    return blocks.reshape(TOKEN_COUNT, TEACHER_Q_HEADS * HEAD_SIZE)

def student_layer(queries, key_rows, value_rows, target):
    heads_of_keys = STUDENT_KV_HEADS
    heads_per_group = STUDENT_Q_HEADS // STUDENT_KV_HEADS
    rows_per_block = math.gcd(TOKEN_COUNT, 256)
    key_grid = key_rows.reshape(TOKEN_COUNT, heads_of_keys, HEAD_SIZE)
    value_grid = value_rows.reshape(TOKEN_COUNT, heads_of_keys, HEAD_SIZE)
    key_pos = jnp.arange(TOKEN_COUNT, dtype=jnp.int32)
    inverse_root = 1.0 / math.sqrt(HEAD_SIZE)

    def query_block(carried, block_index):
        key_gradient, value_gradient = carried
        offset = (block_index * rows_per_block).astype(jnp.int32)
        block_queries = lax.dynamic_slice_in_dim(queries, offset, rows_per_block, 0).reshape(rows_per_block, heads_of_keys, heads_per_group, HEAD_SIZE)
        query_pos = offset + jnp.arange(rows_per_block, dtype=jnp.int32)
        scores, allowed = causal_scores(block_queries, key_grid, query_pos, key_pos)
        row_peak, weights, row_total = softmax_parts(scores, allowed)
        context = attend(weights, row_total, value_grid)
        block_target = lax.dynamic_slice_in_dim(target, offset, rows_per_block, 0).reshape(rows_per_block, heads_of_keys, heads_per_group, HEAD_SIZE).astype(jnp.float32)
        mismatch = context - block_target
        per_token_loss = lax.optimization_barrier(jnp.mean(jnp.square(mismatch).reshape(rows_per_block, -1), axis=1))
        grad_context = reverted(mismatch)
        row_delta = jnp.transpose(lax.optimization_barrier(jnp.sum(mismatch * context, axis=-1)), (1, 2, 0))
        probability = jnp.where(allowed, jnp.exp(scores - row_peak[..., None]) / row_total[..., None], 0.0)
        grad_prob = jnp.einsum('qgjd,kgd->gjqk', grad_context, value_grid.astype(jnp.float32))
        grad_score = reverted(probability * (grad_prob - row_delta[..., None]))
        query_gradient = jnp.einsum('gjqk,kgd->qgjd', grad_score, key_grid.astype(jnp.float32)) * inverse_root
        key_gradient = key_gradient + jnp.einsum('gjqk,qgjd->kgd', grad_score, block_queries.astype(jnp.float32)) * inverse_root
        value_gradient = value_gradient + jnp.einsum('gjqk,qgjd->kgd', reverted(probability), grad_context)
        return ((key_gradient, value_gradient), (query_gradient.reshape(rows_per_block, STUDENT_Q_HEADS * HEAD_SIZE), per_token_loss))
    start_grads = (jnp.zeros((TOKEN_COUNT, heads_of_keys, HEAD_SIZE), jnp.float32), jnp.zeros((TOKEN_COUNT, heads_of_keys, HEAD_SIZE), jnp.float32))
    finals, outputs = lax.scan(query_block, start_grads, jnp.arange(TOKEN_COUNT // rows_per_block, dtype=jnp.int32))
    key_gradient, value_gradient = finals
    query_gradient, per_token_loss = outputs
    return (query_gradient.reshape(TOKEN_COUNT, STUDENT_Q_HEADS * HEAD_SIZE), key_gradient.reshape(TOKEN_COUNT, STUDENT_KV_HEADS * HEAD_SIZE), value_gradient.reshape(TOKEN_COUNT, STUDENT_KV_HEADS * HEAD_SIZE), per_token_loss.reshape(TOKEN_COUNT))

def reference(teacher_query_array, teacher_keys, teacher_value_array, projection, student_query_array, student_keys, student_value_array):
    rows_half = TOKEN_COUNT // 2 // N_SEQ

    def teacher_join(operand):
        return operand.reshape(LAYER_PAIRS, 2, TOKEN_COUNT, -1).transpose(0, 2, 1, 3).reshape(LAYER_PAIRS, TOKEN_COUNT, -1)

    def student_join(operand):
        return operand.reshape(LAYER_PAIRS, 2, N_SEQ, rows_half, -1).transpose(0, 2, 1, 3, 4).reshape(LAYER_PAIRS, TOKEN_COUNT, -1)

    def student_split(operand):
        return operand.reshape(LAYER_PAIRS, N_SEQ, 2, rows_half, -1).transpose(0, 2, 1, 3, 4).reshape(2 * LAYER_PAIRS, TOKEN_COUNT // 2, -1)
    queries_of_teacher = teacher_join(teacher_query_array)
    teacher_key_rows = teacher_join(teacher_keys)
    teacher_value_rows = teacher_join(teacher_value_array)
    queries_of_student = student_join(student_query_array)
    student_key_rows = student_join(student_keys)
    student_value_rows = student_join(student_value_array)
    maps = projection.reshape(LAYER_PAIRS, STUDENT_Q_HEADS, TEACHER_Q_HEADS // STUDENT_Q_HEADS * HEAD_SIZE, HEAD_SIZE)
    results = []
    for layer_index in range(LAYER_PAIRS):
        context = teacher_context(queries_of_teacher[layer_index], teacher_key_rows[layer_index], teacher_value_rows[layer_index])
        target = jnp.einsum('thf,hfe->the', context.reshape(TOKEN_COUNT, STUDENT_Q_HEADS, -1).astype(jnp.float32), maps[layer_index].astype(jnp.float32))
        target = target.astype(jnp.bfloat16).reshape(TOKEN_COUNT, STUDENT_Q_HEADS * HEAD_SIZE)
        results.append(student_layer(queries_of_student[layer_index], student_key_rows[layer_index], student_value_rows[layer_index], target))
    query_gradient = student_split(jnp.stack([entry[0] for entry in results]))
    key_gradient = student_split(jnp.stack([entry[1] for entry in results]))
    value_gradient = student_split(jnp.stack([entry[2] for entry in results]))
    per_token_loss = student_split(jnp.stack([entry[3] for entry in results])[..., None])[..., 0]
    return (query_gradient, key_gradient, value_gradient, per_token_loss)
```

```python
import functools
import math

import jax
import jax.numpy as jnp
from jax import lax
from jax.experimental import pallas as pl
from jax.experimental.pallas import tpu as pltpu
from jax.sharding import PartitionSpec as P

D = 128
NS = 16
TOK = 4096
HALF = TOK // 2
ROOT = 1.0 / math.sqrt(D)
SCALE2 = ROOT * math.log2(math.e)
FLOOR = -1e30
MESH = pl.DeviceIdType.MESH
F32 = jnp.float32
BF16 = jnp.bfloat16


def dot_nt(x, y):
    return lax.dot_general(x, y, (((1,), (1,)), ((), ())), preferred_element_type=F32)


def dot_nn(x, y):
    return lax.dot_general(x, y, (((1,), (0,)), ((), ())), preferred_element_type=F32)


def wide(x, width):
    return x if width == D else jnp.concatenate([x] * (width // D), axis=1)


def absorb(query, keys, values, state, allowed=None):
    peak, acc = state
    scores = dot_nt(query, keys)
    if allowed is not None:
        scores = jnp.where(allowed, scores, FLOOR)
    top = jnp.broadcast_to(jnp.max(scores, axis=1, keepdims=True), peak.shape)
    new = jnp.maximum(peak, top)
    weights = jnp.exp2((scores - wide(new, scores.shape[1])) * SCALE2)
    fade = jnp.exp2((peak - new) * SCALE2)
    acc = acc * wide(fade, 2 * D) + dot_nn(weights.astype(BF16), values)
    return new, acc


def attend(queries, rows_at, key_ref, value_ref, full, rest_start, rest):
    rows = queries[0].shape[0]
    fresh = tuple(
        (jnp.full((rows, D), FLOOR, F32), jnp.zeros((rows, 2 * D), F32)) for _ in queries
    )

    def chunk(index, states):
        start = pl.multiple_of(index * 1024, 1024)
        keys = key_ref[pl.ds(start, 1024), :]
        values = value_ref[pl.ds(start, 1024), :]
        return tuple(absorb(q, keys, values, s) for q, s in zip(queries, states))

    states = lax.fori_loop(0, full, chunk, fresh)
    start = pl.multiple_of(rest_start, 256)
    keys = key_ref[pl.ds(start, rest), :]
    values = value_ref[pl.ds(start, rest), :]
    out = []
    for q, at, s in zip(queries, rows_at, states):
        key_pos = start + lax.broadcasted_iota(jnp.int32, (rows, rest), 1)
        row_pos = at + lax.broadcasted_iota(jnp.int32, (rows, rest), 0)
        out.append(absorb(q, keys, values, s, key_pos <= row_pos))
    return out


def student_forward(half, sq, sk, sv, ctx, lse):
    def group(sg, _):
        for sr in range(4):
            block = sg * 4 + sr
            row = pl.multiple_of(block * 128, 128)
            (peak, acc), = attend(
                [sq[pl.ds(row, 128), :]],
                [block * 256 + half * 128],
                sk, sv, sg, sg * 1024, 256 * (sr + 1),
            )
            total = acc[:, D:]
            ctx[pl.ds(row, 128), :] = acc[:, :D] / total
            log_sum = peak * SCALE2 + jnp.log2(total)
            lse[:, pl.ds(row, 128)] = jnp.transpose(log_sum)[:8, :]
        return 0

    lax.fori_loop(0, 4, group, 0)


def teacher_forward(half, heads, tq, tk, tv, tctx):
    def group(sg, _):
        for sr in range(4):
            block = sg * 4 + sr
            at = block * 256 + half * 128
            done = attend(
                [tq[block, :, h * D : (h + 1) * D] for h in heads],
                [at] * len(heads),
                tk, tv, sg, sg * 1024, 256 * (sr + 1),
            )
            for h, (_, acc) in zip(heads, done):
                tctx[block, :, h * D : (h + 1) * D] = (acc[:, :D] / acc[:, D:]).astype(BF16)
        return 0

    lax.fori_loop(0, 4, group, 0)


def mismatches(tctx, proj, ctx, grad_ctx, delta, loss):
    def step(block, _):
        row = pl.multiple_of(block * 128, 128)
        target = dot_nn(tctx[block], proj[...]).astype(BF16).astype(F32)
        context = ctx[pl.ds(row, 128), :]
        miss = context - target
        grad_ctx[pl.ds(row, 128), :] = miss.astype(BF16)
        dots = jnp.sum(miss * context, axis=1, keepdims=True)
        delta[:, pl.ds(row, 128)] = jnp.transpose(jnp.broadcast_to(dots, (128, 128)))[:8, :]
        squares = jnp.sum(miss * miss, axis=1, keepdims=True) * (1.0 / 2048.0)
        loss[block] = jnp.transpose(jnp.broadcast_to(squares, (128, 128)))[:8, :]
        return 0

    lax.fori_loop(0, NS, step, 0)


KB = 512
QB = 256


def backward(half, first, sq, sk, sv, grad_ctx, lse, delta, dqt, dkv, dq, after):
    dqt[...] = jnp.zeros(dqt.shape, F32)

    def outer(step, _):
        jb = lax.rem(first + step, TOK // KB)
        key_at = pl.multiple_of(jb * KB, KB)
        keys = sk[pl.ds(key_at, KB), :]
        values = sv[pl.ds(key_at, KB), :D]
        keys_t = jnp.transpose(keys)

        def inner(mb, carried, masked):
            dk, dv = carried
            row = pl.multiple_of(mb * QB, QB)
            query = sq[pl.ds(row, QB), :]
            grad = grad_ctx[pl.ds(row, QB), :]
            log_sum = lse[0:1, pl.ds(row, QB)]
            dots = delta[0:1, pl.ds(row, QB)]
            scores = dot_nt(keys, query)
            prob = jnp.exp2(scores * SCALE2 - log_sum)
            if masked:
                key_pos = key_at + lax.broadcasted_iota(jnp.int32, (KB, QB), 0)
                lane = lax.broadcasted_iota(jnp.int32, (KB, QB), 1)
                row_pos = mb * (2 * QB) + lane + half * 128 + jnp.where(lane >= 128, 128, 0)
                prob = jnp.where(key_pos <= row_pos, prob, 0.0)
            grad_prob = dot_nt(values, grad)
            ds = (prob * (grad_prob - dots)).astype(BF16)
            dv = dv + dot_nn(prob.astype(BF16), grad)
            dk = dk + dot_nn(ds, query)
            dqt[:, pl.ds(row, QB)] += dot_nn(keys_t, ds)
            return dk, dv

        zero = jnp.zeros((KB, D), F32)
        carried = inner(jb, (zero, zero), True)
        dk, dv = lax.fori_loop(
            jb + 1, TOK // KB, lambda mb, c: inner(mb, c, False), carried
        )
        dkv[pl.ds(key_at, KB), :D] = (dk * ROOT).astype(BF16)
        dkv[pl.ds(key_at, KB), D:] = dv.astype(BF16)
        after(jb)
        return 0

    lax.fori_loop(0, TOK // KB, outer, 0)

    def turn(block, _):
        row = pl.multiple_of(block * 128, 128)
        dq[pl.ds(row, 128), :] = jnp.transpose(dqt[:, pl.ds(row, 128)]) * ROOT
        return 0

    lax.fori_loop(0, NS, turn, 0)


class Place:
    def __init__(self):
        self.section = lax.axis_index("section")
        self.s = lax.axis_index("seq")
        self.c = lax.rem(self.section, 2)
        self.base = self.section - self.c
        self.half = lax.rem(self.s, 2)
        self.h8 = head_of(self.s)
        self.head = self.c * 8 + self.h8
        self.me = self.c * NS + self.s


def head_of(s):
    return lax.rem(lax.div(s, 2), 4) * 2 + lax.div(s, 8)


def push(here, src, dst, send, recv, c, s):
    same = jnp.logical_and(c == here.c, s == here.s)

    @pl.when(same)
    def _():
        pltpu.make_async_copy(src, dst, recv).start()

    @pl.when(jnp.logical_not(same))
    def _():
        pltpu.make_async_remote_copy(
            src_ref=src, dst_ref=dst, send_sem=send, recv_sem=recv,
            device_id={"section": here.base + c, "seq": s}, device_id_type=MESH,
        ).start()


def greet(here):
    barrier = pltpu.get_barrier_semaphore()

    def signal(t, _):
        other = lax.rem(here.me + t, 2 * NS)
        pl.semaphore_signal(
            barrier, inc=1,
            device_id={"section": here.base + lax.div(other, NS), "seq": lax.rem(other, NS)},
            device_id_type=MESH,
        )
        return 0

    lax.fori_loop(1, 2 * NS, signal, 0)
    pl.semaphore_wait(barrier, 2 * NS - 1)


def drain(ref, sem):
    pltpu.make_async_copy(ref, ref, sem).wait()


S_K, S_V, S_Q, T_K, T_V, T_Q, G_Q, G_KV, LOSS = 0, 1, 2, 3, 4, 5, 9, 10, 11
FWD = 12
N_SEM = 16


def send_student(here, sq, sk, sv, sqb, skb, svb, send, recv):
    def step(t, _):
        chip = lax.rem(here.c * 8 + lax.div(here.s, 2) + t, 16)
        c, p = lax.div(chip, 8), lax.rem(chip, 8)
        h8 = head_of(2 * p)
        kv = pl.multiple_of((2 * c + lax.div(h8, 4)) * D, D)
        q = pl.multiple_of((c * 8 + h8) * D, D)
        at = pl.multiple_of(here.s * 256 + here.c * 128, 128)
        push(here, sk.at[0, :, pl.ds(kv, D)], skb.at[pl.ds(at, 128), :],
             send.at[S_K], recv.at[S_K], c, 2 * p)
        push(here, sv.at[0, :, pl.ds(kv, D)], svb.at[pl.ds(at, 128), pl.ds(0, D)],
             send.at[S_V], recv.at[S_V], c, 2 * p + 1)
        to = pl.multiple_of(here.s * 128, 128)
        push(here, sq.at[0, :, pl.ds(q, D)], sqb.at[pl.ds(to, 128), :],
             send.at[S_Q], recv.at[S_Q], c, 2 * p + here.c)
        return 0

    lax.fori_loop(0, 16, step, 0)


def send_teacher(here, tq, tk, tv, tqb, tkb, tvb, send, recv):
    def step(t, _):
        p = lax.rem(lax.div(here.s, 2) + t, 8)
        kv = pl.multiple_of(lax.div(head_of(2 * p), 2) * D, D)
        at = pl.multiple_of(here.s * 256, 256)
        push(here, tk.at[0, :, pl.ds(kv, D)], tkb.at[pl.ds(at, 256), :],
             send.at[T_K], recv.at[T_K], here.c, 2 * p)
        push(here, tv.at[0, :, pl.ds(kv, D)], tvb.at[pl.ds(at, 256), pl.ds(0, D)],
             send.at[T_V], recv.at[T_V], here.c, 2 * p + 1)
        return 0

    lax.fori_loop(0, 8, step, 0)
    for h in range(4):
        def query(t, _):
            s = lax.rem(here.s + t, NS)
            col = pl.multiple_of(head_of(s) * 512 + h * D, D)
            row = pl.multiple_of(lax.rem(s, 2) * 128, 128)
            push(here, tq.at[0, pl.ds(row, 128), pl.ds(col, D)],
                 tqb.at[here.s, :, pl.ds(h * D, D)],
                 send.at[T_Q + h], recv.at[T_Q + h], here.c, s)
            return 0

        lax.fori_loop(0, NS, query, 0)


def sibling(here, ref, send, recv):
    return pltpu.make_async_remote_copy(
        src_ref=ref, dst_ref=ref, send_sem=send, recv_sem=recv,
        device_id={"section": here.section, "seq": here.s + 1 - 2 * here.half},
        device_id_type=MESH,
    )


def share(here, kb, vb, send, recv, k, v, fk, fv):
    values = vb.at[:, pl.ds(0, D)]

    @pl.when(here.half == 0)
    def _():
        drain(kb, recv.at[k])
        sibling(here, kb, send.at[fk], recv.at[fk]).start()
        drain(values, recv.at[fv])

    @pl.when(here.half == 1)
    def _():
        drain(values, recv.at[v])
        sibling(here, values, send.at[fv], recv.at[fv]).start()
        drain(kb, recv.at[fk])


def kernel(tq, tk, tv, proj, sq, sk, sv, out_q, out_k, out_v, out_loss,
           tqb, tkb, tvb, sqb, skb, svb, projb, ctx, lse, tctx, grad_ctx, delta, loss,
           dqt, dkv, dq, got_kv, got_loss, send, recv, local):
    here = Place()
    own_proj = pltpu.make_async_copy(proj.at[0, here.h8], projb, local)
    own_proj.start()
    greet(here)
    send_student(here, sq, sk, sv, sqb, skb, svb, send, recv)
    send_teacher(here, tq, tk, tv, tqb, tkb, tvb, send, recv)
    svb[:, D:] = jnp.ones((TOK, D), BF16)
    tvb[:, D:] = jnp.ones((TOK, D), BF16)
    share(here, skb, svb, send, recv, S_K, S_V, FWD, FWD + 1)
    drain(sqb, recv.at[S_Q])
    student_forward(here.half, sqb, skb, svb, ctx, lse)
    share(here, tkb, tvb, send, recv, T_K, T_V, FWD + 2, FWD + 3)
    for heads in ((0, 1), (2, 3)):
        for h in heads:
            drain(tqb.at[:, :, pl.ds(h * D, D)], recv.at[T_Q + h])
        teacher_forward(here.half, heads, tqb, tkb, tvb, tctx)
    own_proj.wait()
    mismatches(tctx, projb, ctx, grad_ctx, delta, loss)

    def send_loss(t, _):
        s = lax.rem(here.s + t, NS)
        push(here, loss.at[s], got_loss.at[here.head], send.at[LOSS], recv.at[LOSS], here.half, s)
        return 0

    lax.fori_loop(0, NS, send_loss, 0)
    slot = here.head * 2 + here.half

    def send_kv(jb):
        for e in range(2):
            for c in range(2):
                row = pl.multiple_of(jb * KB + e * 256 + c * 128, 128)
                push(here, dkv.at[pl.ds(row, 128), :], got_kv.at[slot],
                     send.at[G_KV], recv.at[G_KV], c, jb * 2 + e)

    backward(here.half, lax.div(here.s, 2), sqb, skb, svb, grad_ctx, lse, delta, dqt, dkv, dq,
             send_kv)

    def send_q(t, _):
        s = lax.rem(here.s + t, NS)
        row = pl.multiple_of(s * 128, 128)
        col = pl.multiple_of(here.head * D, D)
        push(here, dq.at[pl.ds(row, 128), :], out_q.at[0, :, pl.ds(col, D)],
             send.at[G_Q], recv.at[G_Q], here.half, s)
        return 0

    lax.fori_loop(0, NS, send_q, 0)

    drain(got_loss, recv.at[LOSS])
    total = got_loss[0]
    for h in range(1, 16):
        total = total + got_loss[h]
    out_loss[...] = total[0:1, :]
    drain(got_kv, recv.at[G_KV])
    for g in range(4):
        total = got_kv[g * 8].astype(F32)
        for i in range(1, 8):
            total = total + got_kv[g * 8 + i].astype(F32)
        out_k[0, :, g * D : (g + 1) * D] = total[:, :D]
        out_v[0, :, g * D : (g + 1) * D] = total[:, D:]
    drain(out_q, recv.at[G_Q])

    own_core = here.half == 0

    @pl.when(own_core)
    def _():
        drain(skb.at[pl.ds(0, 15 * 128), :], send.at[S_K])
        drain(svb.at[pl.ds(0, 16 * 128), pl.ds(0, D)], send.at[S_V])
        drain(tkb.at[pl.ds(0, 7 * 256), :], send.at[T_K])
        drain(tvb.at[pl.ds(0, 8 * 256), pl.ds(0, D)], send.at[T_V])
        drain(skb, send.at[FWD])
        drain(tkb, send.at[FWD + 2])

    @pl.when(jnp.logical_not(own_core))
    def _():
        drain(skb.at[pl.ds(0, 16 * 128), :], send.at[S_K])
        drain(svb.at[pl.ds(0, 15 * 128), pl.ds(0, D)], send.at[S_V])
        drain(tkb.at[pl.ds(0, 8 * 256), :], send.at[T_K])
        drain(tvb.at[pl.ds(0, 7 * 256), pl.ds(0, D)], send.at[T_V])
        drain(svb.at[:, pl.ds(0, D)], send.at[FWD + 1])
        drain(tvb.at[:, pl.ds(0, D)], send.at[FWD + 3])

    for h in range(4):
        drain(tqb.at[pl.ds(0, 15), :, pl.ds(h * D, D)], send.at[T_Q + h])
    drain(got_kv.at[pl.ds(0, 31)], send.at[G_KV])
    with_self = here.half == here.c

    @pl.when(with_self)
    def _():
        drain(sqb.at[pl.ds(0, 15 * 128), :], send.at[S_Q])
        drain(dq.at[pl.ds(0, 15 * 128), :], send.at[G_Q])
        drain(loss.at[pl.ds(0, 15)], send.at[LOSS])

    @pl.when(jnp.logical_not(with_self))
    def _():
        drain(sqb, send.at[S_Q])
        drain(dq, send.at[G_Q])
        drain(loss, send.at[LOSS])


def body(tq, tk, tv, proj, sq, sk, sv):
    vmem = pltpu.VMEM
    return pl.pallas_call(
        kernel,
        out_shape=(
            jax.ShapeDtypeStruct((1, 128, 2048), F32),
            jax.ShapeDtypeStruct((1, 128, 512), F32),
            jax.ShapeDtypeStruct((1, 128, 512), F32),
            jax.ShapeDtypeStruct((1, 128), F32),
        ),
        in_specs=[pl.BlockSpec(memory_space=pl.ANY)] * 7,
        out_specs=(
            pl.BlockSpec(memory_space=pl.ANY),
            pl.BlockSpec(memory_space=vmem),
            pl.BlockSpec(memory_space=vmem),
            pl.BlockSpec(memory_space=vmem),
        ),
        scratch_shapes=[
            vmem((NS, 128, 512), BF16),
            vmem((TOK, D), BF16),
            vmem((TOK, 2 * D), BF16),
            vmem((HALF, D), BF16),
            vmem((TOK, D), BF16),
            vmem((TOK, 2 * D), BF16),
            vmem((512, D), BF16),
            vmem((HALF, D), F32),
            vmem((8, HALF), F32),
            vmem((NS, 128, 512), BF16),
            vmem((HALF, D), BF16),
            vmem((8, HALF), F32),
            vmem((NS, 8, 128), F32),
            vmem((D, HALF), F32),
            vmem((TOK, 2 * D), BF16),
            vmem((HALF, D), F32),
            vmem((32, 128, 2 * D), BF16),
            vmem((16, 8, 128), F32),
            pltpu.SemaphoreType.DMA((N_SEM,)),
            pltpu.SemaphoreType.DMA((N_SEM,)),
            pltpu.SemaphoreType.DMA,
        ],
        compiler_params=pltpu.CompilerParams(
            collective_id=0, has_side_effects=True, vmem_limit_bytes=56 * 1024 * 1024
        ),
        cost_estimate=pl.CostEstimate(
            flops=17_000_000_000, bytes_accessed=8_000_000, transcendentals=30_000_000
        ),
    )(tq, tk, tv, proj, sq, sk, sv)


def solution(mesh):
    rows = P("section", "seq", None)
    return jax.shard_map(
        body,
        mesh=mesh,
        in_specs=(rows, rows, rows, P("section", None, None, None), rows, rows, rows),
        out_specs=(rows, rows, rows, P("section", "seq")),
        check_vma=False,
    )
```

```python
import functools
import math

import jax
import jax.numpy as jnp
from jax import lax
from jax.experimental import pallas as pl
from jax.experimental.pallas import tpu as pltpu
from jax.sharding import PartitionSpec as P

D = 128
NS = 16
TOK = 4096
HALF = TOK // 2
ROOT = 1.0 / math.sqrt(D)
SCALE2 = ROOT * math.log2(math.e)
FLOOR = -1e30
MESH = pl.DeviceIdType.MESH
F32 = jnp.float32
BF16 = jnp.bfloat16


def dot_nt(x, y):
    return lax.dot_general(x, y, (((1,), (1,)), ((), ())), preferred_element_type=F32)


def dot_nn(x, y):
    return lax.dot_general(x, y, (((1,), (0,)), ((), ())), preferred_element_type=F32)


KC = 1024
QB = 512


def fold(x, op):
    out = x[:8]
    for i in range(8, x.shape[0], 8):
        out = op(out, x[i : i + 8])
    return out


def position(group, half):
    lane = lax.broadcasted_iota(jnp.int32, (1, QB), 1)
    return group * (2 * QB) + half * 128 + lax.div(lane, 128) * 256 + lax.rem(lane, 128)


class Flash:
    def __init__(self, half, keys, values_t, query, group, finish, score, top, total, acc):
        self.half, self.keys, self.values_t = half, keys, values_t
        self.query, self.group, self.finish = query, group, finish
        self.score, self.top, self.total, self.acc = score, top, total, acc

    def take(self, query, chunk, buf):
        span = pl.ds(pl.multiple_of(chunk * KC, KC), KC)
        scores = dot_nt(self.keys[span, :], query)
        buf[span, :] = scores
        self.top[...] = jnp.maximum(self.top[...], fold(scores, jnp.maximum))

    def take_last(self, query, chunk, buf):
        at = position(chunk, self.half)
        start = pl.multiple_of(chunk * KC, KC)
        low, high = pl.ds(start, 512), pl.ds(pl.multiple_of(start + 512, 512), 512)
        key_pos = start + lax.broadcasted_iota(jnp.int32, (512, 256), 0)
        scores = dot_nt(self.keys[low, :], query)
        near = jnp.where(key_pos <= at[:, :256], scores[:, :256], FLOOR)
        buf[low, :256] = near
        buf[low, 256:] = scores[:, 256:]
        far = dot_nt(self.keys[high, :], query[256:, :])
        far = jnp.where(key_pos + 512 <= at[:, 256:], far, FLOOR)
        buf[high, 256:] = far
        self.top[:, :256] = jnp.maximum(self.top[:, :256], fold(near, jnp.maximum))
        self.top[:, 256:] = jnp.maximum(
            self.top[:, 256:],
            jnp.maximum(fold(scores[:, 256:], jnp.maximum), fold(far, jnp.maximum)),
        )

    def mix(self, peak, chunk, buf):
        span = pl.ds(pl.multiple_of(chunk * KC, KC), KC)
        weights = jnp.exp2((buf[span, :] - peak) * SCALE2)
        self.total[...] += fold(weights, jnp.add)
        self.acc[...] += dot_nn(self.values_t[chunk], weights.astype(BF16))

    def mix_last(self, peak, chunk, buf):
        start = pl.multiple_of(chunk * KC, KC)
        low, high = pl.ds(start, 512), pl.ds(pl.multiple_of(start + 512, 512), 512)
        near = jnp.exp2((buf[low, :] - peak) * SCALE2)
        far = jnp.exp2((buf[high, 256:] - peak[:, 256:]) * SCALE2)
        self.total[...] += fold(near, jnp.add)
        self.total[:, 256:] += fold(far, jnp.add)
        self.acc[...] += dot_nn(self.values_t[chunk, :, :512], near.astype(BF16))
        self.acc[:, 256:] += dot_nn(self.values_t[chunk, :, 512:], far.astype(BF16))

    def turn(self):
        peak = jnp.max(self.top[...], axis=0, keepdims=True)
        self.top[...] = jnp.full((8, QB), FLOOR, F32)
        self.total[...] = jnp.zeros((8, QB), F32)
        self.acc[...] = jnp.zeros((D, QB), F32)
        return peak

    def end(self, task, peak):
        self.finish(task, peak, jnp.sum(self.total[...], axis=0, keepdims=True), self.acc[...])

    def lead(self, task, buf):
        self.top[...] = jnp.full((8, QB), FLOOR, F32)
        query, last = self.query(task), self.group(task)

        def one(chunk, _):
            self.take(query, chunk, buf)
            return 0

        lax.fori_loop(0, last, one, 0)
        self.take_last(query, last, buf)

    def step(self, task, old, new):
        peak = self.turn()
        done, query, last = self.group(task), self.query(task + 1), self.group(task + 1)

        def both(chunk, _):
            self.take(query, chunk, new)
            self.mix(peak, chunk, old)
            return 0

        lax.fori_loop(0, jnp.minimum(last, done), both, 0)

        @pl.when(done > last)
        def _():
            self.take_last(query, last, new)
            self.mix(peak, last, old)
            self.mix_last(peak, done, old)

        @pl.when(done < last)
        def _():
            self.mix_last(peak, done, old)
            self.take(query, done, new)
            self.take_last(query, last, new)

        @pl.when(done == last)
        def _():
            self.take_last(query, last, new)
            self.mix_last(peak, done, old)

        self.end(task, peak)

    def tail(self, task, old):
        peak = self.turn()
        done = self.group(task)

        def rest(chunk, _):
            self.mix(peak, chunk, old)
            return 0

        lax.fori_loop(0, done, rest, 0)
        self.mix_last(peak, done, old)
        self.end(task, peak)

    def run(self, tasks, ready=None):
        if ready is not None:
            ready(0)
        self.lead(0, self.score[0])

        def pair(i, _):
            self.step(2 * i, self.score[0], self.score[1])
            if ready is not None:
                ready(2 * i + 2)
            self.step(2 * i + 1, self.score[1], self.score[0])
            return 0

        lax.fori_loop(0, tasks // 2 - 1, pair, 0)
        self.step(tasks - 2, self.score[0], self.score[1])
        self.tail(tasks - 1, self.score[1])


def columns(group):
    return pl.ds(pl.multiple_of(group * QB, QB), QB)


def student_forward(half, sq, sk, svt, ctx_t, lse, work):
    def finish(task, peak, total, acc):
        at = columns(3 - task)
        ctx_t[:, at] = acc / total
        lse[:, at] = jnp.broadcast_to(peak * SCALE2 + jnp.log2(total), (8, QB))

    Flash(half, sk, svt, lambda t: sq[columns(3 - t), :], lambda t: 3 - t, finish, *work).run(4)


def teacher_forward(half, tq, tk, tvt, tctx_t, work, ready=None):
    def group(task):
        down = 3 - lax.rem(task, 4)
        return jnp.where(lax.rem(lax.div(task, 4), 2) == 0, down, 3 - down)

    def finish(task, peak, total, acc):
        row = pl.multiple_of(lax.div(task, 4) * D, D)
        tctx_t[pl.ds(row, D), columns(group(task))] = (acc / total).astype(BF16)

    Flash(half, tk, tvt, lambda t: tq[lax.div(t, 4), columns(group(t)), :], group, finish,
          *work).run(16, ready)


def turn_values(values, values_t):
    def chunk(i, _):
        values_t[i] = jnp.transpose(values[pl.ds(pl.multiple_of(i * KC, KC), KC), :])
        return 0

    lax.fori_loop(0, TOK // KC, chunk, 0)


def mismatches(tctx_t, proj, ctx_t, grad_t, delta, loss):
    proj_t = jnp.transpose(proj[...])

    def step(group, _):
        at = columns(group)
        target = dot_nn(proj_t, tctx_t[:, at]).astype(BF16).astype(F32)
        context = ctx_t[:, at]
        miss = context - target
        grad_t[:, at] = miss.astype(BF16)
        dots = jnp.sum(fold(miss * context, jnp.add), axis=0, keepdims=True)
        delta[:, at] = jnp.broadcast_to(dots, (8, QB))
        squares = jnp.sum(fold(miss * miss, jnp.add), axis=0, keepdims=True) * (1.0 / 2048.0)
        wide = jnp.broadcast_to(squares, (8, QB))
        for i in range(4):
            loss[group * 4 + i] = wide[:, i * 128 : (i + 1) * 128]
        return 0

    lax.fori_loop(0, HALF // QB, step, 0)


def backward(half, first, sq, sk, sv, grad_t, lse, delta, q_t, dq_t, dk, dv, dkv, dq, after):
    dq_t[...] = jnp.zeros(dq_t.shape, F32)
    q_t[...] = jnp.transpose(sq[...])

    def outer(step, _):
        jb = lax.rem(first + step, TOK // KC)
        start = pl.multiple_of(jb * KC, KC)
        spans = [pl.ds(pl.multiple_of(start + e * 512, 512), 512) for e in range(2)]
        turned = [jnp.transpose(sk[span, :]) for span in spans]
        dk[...] = jnp.zeros(dk.shape, F32)
        dv[...] = jnp.zeros(dv.shape, F32)

        def terms(e, at, mask=None):
            query_t, grad = q_t[:, at], grad_t[:, at]
            prob = jnp.exp2(dot_nn(sk[spans[e], :], query_t) * SCALE2 - lse[0:1, at])
            if mask is not None:
                prob = jnp.where(mask, prob, 0.0)
            ds = (prob * (dot_nn(sv[spans[e], :], grad) - delta[0:1, at])).astype(BF16)
            keys = slice(e * 512, (e + 1) * 512)
            dv[:, keys] += dot_nt(grad, prob.astype(BF16))
            dk[:, keys] += dot_nt(query_t, ds)
            dq_t[:, at] += dot_nn(turned[e], ds)

        key_pos = start + lax.broadcasted_iota(jnp.int32, (512, QB), 0)
        at = position(jb, half)
        terms(0, columns(jb), key_pos <= at)
        late = pl.ds(pl.multiple_of(jb * QB + 256, 256), 256)
        terms(1, late, key_pos[:, 256:] + 512 <= at[:, 256:])

        def full(group, _):
            terms(0, columns(group))
            terms(1, columns(group))
            return 0

        lax.fori_loop(jb + 1, HALF // QB, full, 0)
        for i in range(KC // 128):
            span = slice(i * 128, (i + 1) * 128)
            dkv[jb * 4 + i // 2, i % 2, :D, :] = (dk[:, span] * ROOT).astype(BF16)
            dkv[jb * 4 + i // 2, i % 2, D:, :] = dv[:, span].astype(BF16)
        after(step, jb)
        return 0

    lax.fori_loop(0, TOK // KC, outer, 0)

    def turn(group, _):
        dq[columns(group), :] = (jnp.transpose(dq_t[:, columns(group)]) * ROOT).astype(BF16)
        return 0

    lax.fori_loop(0, HALF // QB, turn, 0)


class Place:
    def __init__(self):
        self.section = lax.axis_index("section")
        self.s = lax.axis_index("seq")
        self.c = lax.rem(self.section, 2)
        self.base = self.section - self.c
        self.half = lax.rem(self.s, 2)
        self.h8 = head_of(self.s)
        self.head = self.c * 8 + self.h8
        self.me = self.c * NS + self.s


def head_of(s):
    return lax.rem(lax.div(s, 2), 4) * 2 + lax.div(s, 8)


def push(here, src, dst, send, recv, c, s):
    same = jnp.logical_and(c == here.c, s == here.s)

    @pl.when(same)
    def _():
        pltpu.make_async_copy(src, dst, recv).start()

    @pl.when(jnp.logical_not(same))
    def _():
        pltpu.make_async_remote_copy(
            src_ref=src, dst_ref=dst, send_sem=send, recv_sem=recv,
            device_id={"section": here.base + c, "seq": s}, device_id_type=MESH,
        ).start()


def greet(here):
    barrier = pltpu.get_barrier_semaphore()

    def signal(t, _):
        other = lax.rem(here.me + t, 2 * NS)
        pl.semaphore_signal(
            barrier, inc=1,
            device_id={"section": here.base + lax.div(other, NS), "seq": lax.rem(other, NS)},
            device_id_type=MESH,
        )
        return 0

    lax.fori_loop(1, 2 * NS, signal, 0)
    pl.semaphore_wait(barrier, 2 * NS - 1)


def drain(ref, sem):
    pltpu.make_async_copy(ref, ref, sem).wait()


S_K, S_V, S_Q, T_K, T_V, T_Q, G_Q, G_KV, LOSS = 0, 1, 2, 3, 4, 5, 9, 10, 11
FWD = 12
PAIR = 16
N_SEM = 20


def send_student(here, sq, sk, sv, sqb, skb, svb, send, recv):
    def step(t, _):
        chip = lax.rem(here.c * 8 + lax.div(here.s, 2) + t, 16)
        c, p = lax.div(chip, 8), lax.rem(chip, 8)
        h8 = head_of(2 * p)
        kv = pl.multiple_of((2 * c + lax.div(h8, 4)) * D, D)
        q = pl.multiple_of((c * 8 + h8) * D, D)
        at = pl.multiple_of(here.s * 256 + here.c * 128, 128)
        push(here, sk.at[0, :, pl.ds(kv, D)], skb.at[pl.ds(at, 128), :],
             send.at[S_K], recv.at[S_K], c, 2 * p)
        push(here, sv.at[0, :, pl.ds(kv, D)], svb.at[pl.ds(at, 128), :],
             send.at[S_V], recv.at[S_V], c, 2 * p + 1)
        to = pl.multiple_of(here.s * 128, 128)
        push(here, sq.at[0, :, pl.ds(q, D)], sqb.at[pl.ds(to, 128), :],
             send.at[S_Q], recv.at[S_Q], c, 2 * p + here.c)
        return 0

    lax.fori_loop(0, 16, step, 0)


def send_teacher(here, tq, tk, tv, tqb, tkb, tvb, send, recv):
    def step(t, _):
        p = lax.rem(lax.div(here.s, 2) + t, 8)
        kv = pl.multiple_of(lax.div(head_of(2 * p), 2) * D, D)
        at = pl.multiple_of(here.s * 256, 256)
        push(here, tk.at[0, :, pl.ds(kv, D)], tkb.at[pl.ds(at, 256), :],
             send.at[T_K], recv.at[T_K], here.c, 2 * p)
        push(here, tv.at[0, :, pl.ds(kv, D)], tvb.at[pl.ds(at, 256), :],
             send.at[T_V], recv.at[T_V], here.c, 2 * p + 1)
        return 0

    lax.fori_loop(0, 8, step, 0)
    for h in range(4):
        def query(t, _):
            s = lax.rem(here.s + t, NS)
            col = pl.multiple_of(head_of(s) * 512 + h * D, D)
            row = pl.multiple_of(lax.rem(s, 2) * 128, 128)
            push(here, tq.at[0, pl.ds(row, 128), pl.ds(col, D)],
                 tqb.at[h, pl.ds(pl.multiple_of(here.s * 128, 128), 128), :],
                 send.at[T_Q + h], recv.at[T_Q + h], here.c, s)
            return 0

        lax.fori_loop(0, NS, query, 0)


def sibling(here, src, dst, send, recv):
    return pltpu.make_async_remote_copy(
        src_ref=src, dst_ref=dst, send_sem=send, recv_sem=recv,
        device_id={"section": here.section, "seq": here.s + 1 - 2 * here.half},
        device_id_type=MESH,
    )


def share(here, kb, vb, send, recv, k, v, fk, fv):
    @pl.when(here.half == 0)
    def _():
        drain(kb, recv.at[k])
        sibling(here, kb, kb, send.at[fk], recv.at[fk]).start()
        drain(vb, recv.at[fv])

    @pl.when(here.half == 1)
    def _():
        drain(vb, recv.at[v])
        sibling(here, vb, vb, send.at[fv], recv.at[fv]).start()
        drain(kb, recv.at[fk])


def kernel(tq, tk, tv, proj, sq, sk, sv, out_q, out_k, out_v, out_loss,
           tqb, tkb, tvb, tvt, sqb, skb, svb, svt, projb, ctx_t, lse, tctx_t, grad_t, delta, loss,
           q_t, dq_t, dk, dv, dkv, paired, summed, dq, got_kv, got_loss,
           score0, score1, top, total, acc, send, recv, local):
    here = Place()
    work = ((score0, score1), top, total, acc)
    own_proj = pltpu.make_async_copy(proj.at[0, here.h8], projb, local)
    own_proj.start()
    greet(here)
    send_student(here, sq, sk, sv, sqb, skb, svb, send, recv)
    send_teacher(here, tq, tk, tv, tqb, tkb, tvb, send, recv)
    share(here, skb, svb, send, recv, S_K, S_V, FWD, FWD + 1)
    turn_values(svb, svt)
    drain(sqb, recv.at[S_Q])
    student_forward(here.half, sqb, skb, svt, ctx_t, lse, work)
    share(here, tkb, tvb, send, recv, T_K, T_V, FWD + 2, FWD + 3)
    turn_values(tvb, tvt)

    def ready(task):
        head = lax.div(task, 4)

        @pl.when(lax.rem(task, 4) == 0)
        def _():
            drain(tqb.at[head], recv.at[T_Q + head])

    teacher_forward(here.half, tqb, tkb, tvt, tctx_t, work, ready)
    own_proj.wait()
    mismatches(tctx_t, projb, ctx_t, grad_t, delta, loss)

    def send_loss(t, _):
        s = lax.rem(here.s + t, NS)
        push(here, loss.at[s], got_loss.at[here.head], send.at[LOSS], recv.at[LOSS], here.half, s)
        return 0

    lax.fori_loop(0, NS, send_loss, 0)
    first = lax.rem(lax.div(here.s, 2), 4)

    def finish_kv(step):
        jb = lax.rem(first + step, 4)
        drain(paired.at[step], recv.at[PAIR + step])

        def one(i, _):
            s = jb * 4 + i
            mine = dkv[s, here.half].astype(F32) + paired[step, i].astype(F32)
            summed[s] = mine.astype(BF16)
            push(here, summed.at[s], got_kv.at[here.head], send.at[G_KV], recv.at[G_KV],
                 here.half, s)
            return 0

        lax.fori_loop(0, 4, one, 0)

    def after(step, jb):
        sibling(here, dkv.at[pl.ds(jb * 4, 4), 1 - here.half], paired.at[step],
                send.at[PAIR], recv.at[PAIR + step]).start()

        @pl.when(step > 0)
        def _():
            finish_kv(step - 1)

    backward(here.half, first, sqb, skb, svb, grad_t, lse, delta, q_t, dq_t, dk, dv, dkv, dq, after)

    def send_q(t, _):
        s = lax.rem(here.s + t, NS)
        row = pl.multiple_of(s * 128, 128)
        col = pl.multiple_of(here.head * D, D)
        push(here, dq.at[pl.ds(row, 128), :], out_q.at[0, :, pl.ds(col, D)],
             send.at[G_Q], recv.at[G_Q], here.half, s)
        return 0

    finish_kv(3)
    lax.fori_loop(0, NS, send_q, 0)

    drain(got_loss, recv.at[LOSS])
    sums = got_loss[0]
    for h in range(1, 16):
        sums = sums + got_loss[h]
    out_loss[...] = sums[0:1, :]
    drain(got_kv, recv.at[G_KV])
    for g in range(4):
        sums = got_kv[g * 4].astype(F32)
        for i in range(1, 4):
            sums = sums + got_kv[g * 4 + i].astype(F32)
        out_k[0, :, g * D : (g + 1) * D] = jnp.transpose(sums[:D])
        out_v[0, :, g * D : (g + 1) * D] = jnp.transpose(sums[D:])
    drain(out_q, recv.at[G_Q])

    own_core = here.half == 0

    @pl.when(own_core)
    def _():
        drain(skb.at[pl.ds(0, 15 * 128), :], send.at[S_K])
        drain(svb.at[pl.ds(0, 16 * 128), :], send.at[S_V])
        drain(tkb.at[pl.ds(0, 7 * 256), :], send.at[T_K])
        drain(tvb.at[pl.ds(0, 8 * 256), :], send.at[T_V])
        drain(skb, send.at[FWD])
        drain(tkb, send.at[FWD + 2])

    @pl.when(jnp.logical_not(own_core))
    def _():
        drain(skb.at[pl.ds(0, 16 * 128), :], send.at[S_K])
        drain(svb.at[pl.ds(0, 15 * 128), :], send.at[S_V])
        drain(tkb.at[pl.ds(0, 8 * 256), :], send.at[T_K])
        drain(tvb.at[pl.ds(0, 7 * 256), :], send.at[T_V])
        drain(svb, send.at[FWD + 1])
        drain(tvb, send.at[FWD + 3])

    for h in range(4):
        drain(tqb.at[h, pl.ds(0, 15 * 128), :], send.at[T_Q + h])
    drain(paired, send.at[PAIR])
    with_self = here.half == here.c

    @pl.when(with_self)
    def _():
        drain(sqb.at[pl.ds(0, 15 * 128), :], send.at[S_Q])
        drain(dq.at[pl.ds(0, 15 * 128), :], send.at[G_Q])
        drain(loss.at[pl.ds(0, 15)], send.at[LOSS])
        drain(got_kv.at[pl.ds(0, 15)], send.at[G_KV])

    @pl.when(jnp.logical_not(with_self))
    def _():
        drain(sqb, send.at[S_Q])
        drain(dq, send.at[G_Q])
        drain(loss, send.at[LOSS])
        drain(got_kv, send.at[G_KV])


def body(tq, tk, tv, proj, sq, sk, sv):
    vmem = pltpu.VMEM
    dq, dk, dv, loss = pl.pallas_call(
        kernel,
        out_shape=(
            jax.ShapeDtypeStruct((1, 128, 2048), BF16),
            jax.ShapeDtypeStruct((1, 128, 512), F32),
            jax.ShapeDtypeStruct((1, 128, 512), F32),
            jax.ShapeDtypeStruct((1, 128), F32),
        ),
        in_specs=[pl.BlockSpec(memory_space=pl.ANY)] * 7,
        out_specs=(
            pl.BlockSpec(memory_space=pl.ANY),
            pl.BlockSpec(memory_space=vmem),
            pl.BlockSpec(memory_space=vmem),
            pl.BlockSpec(memory_space=vmem),
        ),
        scratch_shapes=[
            vmem((4, HALF, D), BF16),
            vmem((TOK, D), BF16),
            vmem((TOK, D), BF16),
            vmem((TOK // KC, D, KC), BF16),
            vmem((HALF, D), BF16),
            vmem((TOK, D), BF16),
            vmem((TOK, D), BF16),
            vmem((TOK // KC, D, KC), BF16),
            vmem((512, D), BF16),
            vmem((D, HALF), F32),
            vmem((8, HALF), F32),
            vmem((4 * D, HALF), BF16),
            vmem((D, HALF), BF16),
            vmem((8, HALF), F32),
            vmem((NS, 8, 128), F32),
            vmem((D, HALF), BF16),
            vmem((D, HALF), F32),
            vmem((D, KC), F32),
            vmem((D, KC), F32),
            vmem((NS, 2, 2 * D, 128), BF16),
            vmem((4, 4, 2 * D, 128), BF16),
            vmem((NS, 2 * D, 128), BF16),
            vmem((HALF, D), BF16),
            vmem((NS, 2 * D, 128), BF16),
            vmem((NS, 8, 128), F32),
            vmem((TOK, QB), F32),
            vmem((TOK, QB), F32),
            vmem((8, QB), F32),
            vmem((8, QB), F32),
            vmem((D, QB), F32),
            pltpu.SemaphoreType.DMA((N_SEM,)),
            pltpu.SemaphoreType.DMA((N_SEM,)),
            pltpu.SemaphoreType.DMA,
        ],
        compiler_params=pltpu.CompilerParams(
            collective_id=0, has_side_effects=True, vmem_limit_bytes=56 * 1024 * 1024
        ),
        cost_estimate=pl.CostEstimate(
            flops=17_000_000_000, bytes_accessed=8_000_000, transcendentals=30_000_000
        ),
    )(tq, tk, tv, proj, sq, sk, sv)
    return dq.astype(F32), dk, dv, loss


def solution(mesh):
    rows = P("section", "seq", None)
    return jax.shard_map(
        body,
        mesh=mesh,
        in_specs=(rows, rows, rows, P("section", None, None, None), rows, rows, rows),
        out_specs=(rows, rows, rows, P("section", "seq")),
        check_vma=False,
    )
```

```python
import functools
import math

import jax
import jax.numpy as jnp
from jax import lax
from jax.experimental import pallas as pl
from jax.experimental.pallas import tpu as pltpu
from jax.sharding import PartitionSpec as P

D = 128
NS = 16
TOK = 4096
HALF = TOK // 2
ROOT = 1.0 / math.sqrt(D)
SCALE2 = ROOT * math.log2(math.e)
FLOOR = -1e30
MESH = pl.DeviceIdType.MESH
F32 = jnp.float32
BF16 = jnp.bfloat16


def dot_nt(x, y):
    return lax.dot_general(x, y, (((1,), (1,)), ((), ())), preferred_element_type=F32)


def dot_nn(x, y):
    return lax.dot_general(x, y, (((1,), (0,)), ((), ())), preferred_element_type=F32)


KC = 1024
QB = 512


def fold(x, op):
    out = x[:8]
    for i in range(8, x.shape[0], 8):
        out = op(out, x[i : i + 8])
    return out


def position(group, half):
    lane = lax.broadcasted_iota(jnp.int32, (1, QB), 1)
    return group * (2 * QB) + half * 128 + lax.div(lane, 128) * 256 + lax.rem(lane, 128)


class Flash:
    def __init__(self, half, keys, values_t, finish, top):
        self.half, self.keys, self.values_t, self.finish, self.top = half, keys, values_t, finish, top

    def take(self, top, query, chunk, buf):
        span = slice(chunk * KC, (chunk + 1) * KC)
        scores = dot_nt(self.keys[span, :], query)
        buf[span, :] = scores
        return jnp.maximum(top, fold(scores, jnp.maximum))

    def take_last(self, top, query, chunk, buf):
        at = position(chunk, self.half)
        start = chunk * KC
        low, high = slice(start, start + 512), slice(start + 512, start + 1024)
        key_pos = start + lax.broadcasted_iota(jnp.int32, (512, 256), 0)
        scores = dot_nt(self.keys[low, :], query)
        far = dot_nt(self.keys[high, :], query[256:, :])
        near = jnp.where(key_pos <= at[:, :256], scores[:, :256], FLOOR)
        far = jnp.where(key_pos + 512 <= at[:, 256:], far, FLOOR)
        buf[low, :256] = near
        buf[low, 256:] = scores[:, 256:]
        buf[high, 256:] = far
        right = jnp.maximum(fold(scores[:, 256:], jnp.maximum), fold(far, jnp.maximum))
        return jnp.maximum(top, jnp.concatenate([fold(near, jnp.maximum), right], axis=1))

    def mix(self, state, peak, chunk, buf):
        total, acc = state
        weights = jnp.exp2((buf[chunk * KC : (chunk + 1) * KC, :] - peak) * SCALE2)
        total = total + fold(weights, jnp.add)
        return total, acc + dot_nn(self.values_t[chunk], weights.astype(BF16))

    def mix_last(self, state, peak, chunk, buf):
        total, acc = state
        start = chunk * KC
        near = jnp.exp2((buf[start : start + 512, :] - peak) * SCALE2)
        far = jnp.exp2((buf[start + 512 : start + 1024, 256:] - peak[:, 256:]) * SCALE2)
        sums = fold(near, jnp.add)
        total = total + jnp.concatenate(
            [sums[:, :256], sums[:, 256:] + fold(far, jnp.add)], axis=1
        )
        near = dot_nn(self.values_t[chunk, :, :512], near.astype(BF16))
        far = dot_nn(self.values_t[chunk, :, 512:], far.astype(BF16))
        return total, acc + jnp.concatenate([near[:, :256], near[:, 256:] + far], axis=1)

    def step(self, task, old, following, new):
        peak = top = None
        state = (jnp.zeros((8, QB), F32), jnp.zeros((D, QB), F32))
        mixes, takes = [], []
        if task is not None:
            peak = jnp.max(self.top[...], axis=0, keepdims=True)
            mixes = list(range(task[0] + 1))
        if following is not None:
            query = following[1]()
            top = jnp.full((8, QB), FLOOR, F32)
            takes = list(range(following[0] + 1))
        for chunk in range(max(len(mixes), len(takes))):
            if chunk < len(takes):
                step = self.take_last if chunk == following[0] else self.take
                top = step(top, query, chunk, new)
            if chunk < len(mixes):
                step = self.mix_last if chunk == task[0] else self.mix
                state = step(state, peak, chunk, old)
        if following is not None:
            self.top[...] = top
        if task is not None:
            task[2](peak, jnp.sum(state[0], axis=0, keepdims=True), state[1])


def columns(group):
    if isinstance(group, int):
        return slice(group * QB, (group + 1) * QB)
    return pl.ds(pl.multiple_of(group * QB, QB), QB)


def student_forward(half, sq, sk, svt, ctx_t, lse, work):
    score, top = work
    flash = Flash(half, sk, svt, None, top)

    def task(group):
        at = columns(group)

        def finish(peak, total, acc):
            ctx_t[:, at] = acc / total
            lse[:, at] = jnp.broadcast_to(peak * SCALE2 + jnp.log2(total), (8, QB))

        return group, lambda: sq[at, :], finish

    tasks = [task(group) for group in (3, 2, 1, 0)]
    flash.step(None, None, tasks[0], score[0])
    for k in range(4):
        following = tasks[k + 1] if k < 3 else None
        flash.step(tasks[k], score[k % 2], following, score[(k + 1) % 2])


def teacher_forward(half, tq, tk, tvt, tctx_t, work, ready):
    score, top = work
    flash = Flash(half, tk, tvt, None, top)

    def task(head, group):
        at = columns(group)

        def finish(peak, total, acc):
            row = pl.multiple_of(head * D, D)
            tctx_t[pl.ds(row, D), at] = (acc / total).astype(BF16)

        return group, lambda: tq[head, at, :], finish

    ready(0)
    flash.step(None, None, task(0, 3), score[0])

    def pair(i, _):
        tasks = [task(2 * i, group) for group in (3, 2, 1, 0)]
        tasks += [task(2 * i + 1, group) for group in (0, 1, 2, 3)]
        for k in range(7):
            if k == 3:
                ready(2 * i + 1)
            flash.step(tasks[k], score[k % 2], tasks[k + 1], score[(k + 1) % 2])

        @pl.when(i == 0)
        def _():
            ready(2)
            flash.step(tasks[7], score[1], task(2, 3), score[0])

        @pl.when(i == 1)
        def _():
            flash.step(tasks[7], score[1], None, None)

        return 0

    lax.fori_loop(0, 2, pair, 0)


def turn_values(values, values_t):
    def chunk(i, _):
        values_t[i] = jnp.transpose(values[pl.ds(pl.multiple_of(i * KC, KC), KC), :])
        return 0

    lax.fori_loop(0, TOK // KC, chunk, 0)


def mismatches(tctx_t, proj, ctx_t, grad_t, delta, loss):
    proj_t = jnp.transpose(proj[...])

    def step(group, _):
        at = columns(group)
        target = dot_nn(proj_t, tctx_t[:, at]).astype(BF16).astype(F32)
        context = ctx_t[:, at]
        miss = context - target
        grad_t[:, at] = miss.astype(BF16)
        dots = jnp.sum(fold(miss * context, jnp.add), axis=0, keepdims=True)
        delta[:, at] = jnp.broadcast_to(dots, (8, QB))
        squares = jnp.sum(fold(miss * miss, jnp.add), axis=0, keepdims=True) * (1.0 / 2048.0)
        wide = jnp.broadcast_to(squares, (8, QB))
        for i in range(4):
            loss[group * 4 + i] = wide[:, i * 128 : (i + 1) * 128]
        return 0

    lax.fori_loop(0, HALF // QB, step, 0)


def backward(half, first, sq, sk, sv, grad_t, lse, delta, q_t, dq_t, dk, dv, dkv, dq, middle, after, send_dq):
    dq_t[...] = jnp.zeros(dq_t.shape, F32)
    q_t[...] = jnp.transpose(sq[...])

    def outer(step, _):
        jb = lax.rem(first + step, TOK // KC)
        start = pl.multiple_of(jb * KC, KC)
        spans = [pl.ds(pl.multiple_of(start + e * 512, 512), 512) for e in range(2)]
        turned = [jnp.transpose(sk[span, :]) for span in spans]
        dk[...] = jnp.zeros(dk.shape, F32)
        dv[...] = jnp.zeros(dv.shape, F32)

        def terms(e, at, mask=None):
            query_t, grad = q_t[:, at], grad_t[:, at]
            prob = jnp.exp2(dot_nn(sk[spans[e], :], query_t) * SCALE2 - lse[0:1, at])
            if mask is not None:
                prob = jnp.where(mask, prob, 0.0)
            ds = (prob * (dot_nn(sv[spans[e], :], grad) - delta[0:1, at])).astype(BF16)
            keys = slice(e * 512, (e + 1) * 512)
            dv[:, keys] += dot_nt(grad, prob.astype(BF16))
            dk[:, keys] += dot_nt(query_t, ds)
            dq_t[:, at] += dot_nn(turned[e], ds)

        key_pos = start + lax.broadcasted_iota(jnp.int32, (512, QB), 0)
        at = position(jb, half)
        terms(0, columns(jb), key_pos <= at)
        late = pl.ds(pl.multiple_of(jb * QB + 256, 256), 256)
        terms(1, late, key_pos[:, 256:] + 512 <= at[:, 256:])

        def leave(group):
            at = columns(group)
            dq[at, :] = (jnp.transpose(dq_t[:, at]) * ROOT).astype(BF16)
            send_dq(group)

        middle(step)

        @pl.when(jnp.logical_or(step + first >= TOK // KC, jnp.logical_and(first == 0, step >= 0)))
        def _():
            leave(jb)

        def full(group, _):
            terms(0, columns(group))
            terms(1, columns(group))

            @pl.when(jnp.logical_and(step == TOK // KC - 1, first > 0))
            def _():
                leave(group)

            return 0

        lax.fori_loop(jb + 1, HALF // QB, full, 0)
        for i in range(KC // 128):
            span = slice(i * 128, (i + 1) * 128)
            dkv[jb * 4 + i // 2, i % 2, :D, :] = (dk[:, span] * ROOT).astype(BF16)
            dkv[jb * 4 + i // 2, i % 2, D:, :] = dv[:, span].astype(BF16)
        after(step, jb)
        return 0

    lax.fori_loop(0, TOK // KC, outer, 0)


class Place:
    def __init__(self):
        self.section = lax.axis_index("section")
        self.s = lax.axis_index("seq")
        self.c = lax.rem(self.section, 2)
        self.base = self.section - self.c
        self.half = lax.rem(self.s, 2)
        self.h8 = head_of(self.s)
        self.head = self.c * 8 + self.h8
        self.me = self.c * NS + self.s


def head_of(s):
    return lax.rem(lax.div(s, 2), 4) * 2 + lax.div(s, 8)


def push(here, src, dst, send, recv, c, s):
    same = jnp.logical_and(c == here.c, s == here.s)

    @pl.when(same)
    def _():
        pltpu.make_async_copy(src, dst, recv).start()

    @pl.when(jnp.logical_not(same))
    def _():
        pltpu.make_async_remote_copy(
            src_ref=src, dst_ref=dst, send_sem=send, recv_sem=recv,
            device_id={"section": here.base + c, "seq": s}, device_id_type=MESH,
        ).start()


def greet(here):
    barrier = pltpu.get_barrier_semaphore()

    def signal(t, _):
        other = lax.rem(here.me + t, 2 * NS)
        pl.semaphore_signal(
            barrier, inc=1,
            device_id={"section": here.base + lax.div(other, NS), "seq": lax.rem(other, NS)},
            device_id_type=MESH,
        )
        return 0

    lax.fori_loop(1, 2 * NS, signal, 0)
    pl.semaphore_wait(barrier, 2 * NS - 1)


def drain(ref, sem):
    pltpu.make_async_copy(ref, ref, sem).wait()


S_K, S_V, S_Q, T_K, T_V, T_Q, G_Q, G_KV, LOSS = 0, 1, 2, 3, 4, 5, 9, 10, 11
FWD = 12
PAIR = 16
N_SEM = 20


def send_student(here, sq, sk, sv, sqb, skb, svb, send, recv):
    def step(t, _):
        chip = lax.rem(here.c * 8 + lax.div(here.s, 2) + jnp.where(here.half == 0, t, 16 - t), 16)
        c, p = lax.div(chip, 8), lax.rem(chip, 8)
        h8 = head_of(2 * p)
        kv = pl.multiple_of((2 * c + lax.div(h8, 4)) * D, D)
        q = pl.multiple_of((c * 8 + h8) * D, D)
        at = pl.multiple_of(here.s * 256 + here.c * 128, 128)
        push(here, sk.at[0, :, pl.ds(kv, D)], skb.at[pl.ds(at, 128), :],
             send.at[S_K], recv.at[S_K], c, 2 * p)
        push(here, sv.at[0, :, pl.ds(kv, D)], svb.at[pl.ds(at, 128), :],
             send.at[S_V], recv.at[S_V], c, 2 * p + 1)
        to = pl.multiple_of(here.s * 128, 128)
        push(here, sq.at[0, :, pl.ds(q, D)], sqb.at[pl.ds(to, 128), :],
             send.at[S_Q], recv.at[S_Q], c, 2 * p + here.c)
        return 0

    lax.fori_loop(0, 16, step, 0)


def send_teacher(here, tq, tk, tv, tqb, tkb, tvb, send, recv):
    def step(t, _):
        p = lax.rem(lax.div(here.s, 2) + jnp.where(here.half == 0, t, 8 - t), 8)
        kv = pl.multiple_of(lax.div(head_of(2 * p), 2) * D, D)
        at = pl.multiple_of(here.s * 256, 256)
        push(here, tk.at[0, :, pl.ds(kv, D)], tkb.at[pl.ds(at, 256), :],
             send.at[T_K], recv.at[T_K], here.c, 2 * p)
        push(here, tv.at[0, :, pl.ds(kv, D)], tvb.at[pl.ds(at, 256), :],
             send.at[T_V], recv.at[T_V], here.c, 2 * p + 1)
        return 0

    lax.fori_loop(0, 8, step, 0)
    for h in range(4):
        def query(t, _):
            p = lax.rem(lax.div(here.s, 2) + jnp.where(here.half == 0, t, 8 - t), 8)
            col = pl.multiple_of(head_of(2 * p) * 512 + h * D, D)
            for core in range(2):
                push(here, tq.at[0, pl.ds(core * 128, 128), pl.ds(col, D)],
                     tqb.at[h, pl.ds(pl.multiple_of(here.s * 128, 128), 128), :],
                     send.at[T_Q + h], recv.at[T_Q + h], here.c, 2 * p + core)
            return 0

        lax.fori_loop(0, 8, query, 0)


def sibling(here, src, dst, send, recv):
    return pltpu.make_async_remote_copy(
        src_ref=src, dst_ref=dst, send_sem=send, recv_sem=recv,
        device_id={"section": here.section, "seq": here.s + 1 - 2 * here.half},
        device_id_type=MESH,
    )


def share(here, kb, vb, send, recv, k, v, fk, fv):
    @pl.when(here.half == 0)
    def _():
        drain(kb, recv.at[k])
        sibling(here, kb, kb, send.at[fk], recv.at[fk]).start()
        drain(vb, recv.at[fv])

    @pl.when(here.half == 1)
    def _():
        drain(vb, recv.at[v])
        sibling(here, vb, vb, send.at[fv], recv.at[fv]).start()
        drain(kb, recv.at[fk])


def kernel(tq, tk, tv, proj, sq, sk, sv, out_q, out_k, out_v, out_loss,
           tqb, tkb, tvb, tvt, sqb, skb, svb, svt, projb, ctx_t, lse, tctx_t, grad_t, delta, loss,
           q_t, dq_t, dk, dv, dkv, paired, summed, dq, got_kv, got_loss,
           score0, score1, top, send, recv, local):
    here = Place()
    work = ((score0, score1), top)
    own_proj = pltpu.make_async_copy(proj.at[0, here.h8], projb, local)
    own_proj.start()
    greet(here)
    send_student(here, sq, sk, sv, sqb, skb, svb, send, recv)
    send_teacher(here, tq, tk, tv, tqb, tkb, tvb, send, recv)
    share(here, skb, svb, send, recv, S_K, S_V, FWD, FWD + 1)
    turn_values(svb, svt)
    drain(sqb, recv.at[S_Q])
    student_forward(here.half, sqb, skb, svt, ctx_t, lse, work)
    share(here, tkb, tvb, send, recv, T_K, T_V, FWD + 2, FWD + 3)
    turn_values(tvb, tvt)

    def ready(head):
        drain(tqb.at[head], recv.at[T_Q + head])

    teacher_forward(here.half, tqb, tkb, tvt, tctx_t, work, ready)
    own_proj.wait()
    mismatches(tctx_t, projb, ctx_t, grad_t, delta, loss)

    def send_loss(t, _):
        s = lax.rem(here.s + t, NS)
        push(here, loss.at[s], got_loss.at[here.head], send.at[LOSS], recv.at[LOSS], here.half, s)
        return 0

    lax.fori_loop(0, NS, send_loss, 0)
    first = lax.rem(lax.div(here.s, 2), 4)

    def finish_kv(step):
        jb = lax.rem(first + step, 4)
        drain(paired.at[step], recv.at[PAIR + step])

        def one(i, _):
            s = jb * 4 + i
            mine = dkv[s, here.half].astype(F32) + paired[step, i].astype(F32)
            summed[s] = mine.astype(BF16)
            push(here, summed.at[s], got_kv.at[here.head], send.at[G_KV], recv.at[G_KV],
                 here.half, s)
            return 0

        lax.fori_loop(0, 4, one, 0)

    def after(step, jb):
        sibling(here, dkv.at[pl.ds(jb * 4, 4), 1 - here.half], paired.at[step],
                send.at[PAIR], recv.at[PAIR + step]).start()

    def middle(step):
        @pl.when(step > 0)
        def _():
            finish_kv(step - 1)

    def send_dq(group):
        def one(i, _):
            s = group * 4 + i
            row = pl.multiple_of(s * 128, 128)
            col = pl.multiple_of(here.head * D, D)
            push(here, dq.at[pl.ds(row, 128), :], out_q.at[0, :, pl.ds(col, D)],
                 send.at[G_Q], recv.at[G_Q], here.half, s)
            return 0

        lax.fori_loop(0, 4, one, 0)

    backward(here.half, first, sqb, skb, svb, grad_t, lse, delta, q_t, dq_t, dk, dv, dkv, dq,
             middle, after, send_dq)
    finish_kv(3)

    drain(got_loss, recv.at[LOSS])
    sums = got_loss[0]
    for h in range(1, 16):
        sums = sums + got_loss[h]
    out_loss[...] = sums[0:1, :]
    drain(got_kv, recv.at[G_KV])
    for g in range(4):
        sums = got_kv[g * 4].astype(F32)
        for i in range(1, 4):
            sums = sums + got_kv[g * 4 + i].astype(F32)
        out_k[0, :, g * D : (g + 1) * D] = jnp.transpose(sums[:D])
        out_v[0, :, g * D : (g + 1) * D] = jnp.transpose(sums[D:])
    drain(out_q, recv.at[G_Q])

    own_core = here.half == 0

    @pl.when(own_core)
    def _():
        drain(skb.at[pl.ds(0, 15 * 128), :], send.at[S_K])
        drain(svb.at[pl.ds(0, 16 * 128), :], send.at[S_V])
        drain(tkb.at[pl.ds(0, 7 * 256), :], send.at[T_K])
        drain(tvb.at[pl.ds(0, 8 * 256), :], send.at[T_V])
        drain(skb, send.at[FWD])
        drain(tkb, send.at[FWD + 2])

    @pl.when(jnp.logical_not(own_core))
    def _():
        drain(skb.at[pl.ds(0, 16 * 128), :], send.at[S_K])
        drain(svb.at[pl.ds(0, 15 * 128), :], send.at[S_V])
        drain(tkb.at[pl.ds(0, 8 * 256), :], send.at[T_K])
        drain(tvb.at[pl.ds(0, 7 * 256), :], send.at[T_V])
        drain(svb, send.at[FWD + 1])
        drain(tvb, send.at[FWD + 3])

    for h in range(4):
        drain(tqb.at[h, pl.ds(0, 15 * 128), :], send.at[T_Q + h])
    drain(paired, send.at[PAIR])
    with_self = here.half == here.c

    @pl.when(with_self)
    def _():
        drain(sqb.at[pl.ds(0, 15 * 128), :], send.at[S_Q])
        drain(dq.at[pl.ds(0, 15 * 128), :], send.at[G_Q])
        drain(loss.at[pl.ds(0, 15)], send.at[LOSS])
        drain(got_kv.at[pl.ds(0, 15)], send.at[G_KV])

    @pl.when(jnp.logical_not(with_self))
    def _():
        drain(sqb, send.at[S_Q])
        drain(dq, send.at[G_Q])
        drain(loss, send.at[LOSS])
        drain(got_kv, send.at[G_KV])


def body(tq, tk, tv, proj, sq, sk, sv):
    vmem = pltpu.VMEM
    dq, dk, dv, loss = pl.pallas_call(
        kernel,
        out_shape=(
            jax.ShapeDtypeStruct((1, 128, 2048), BF16),
            jax.ShapeDtypeStruct((1, 128, 512), F32),
            jax.ShapeDtypeStruct((1, 128, 512), F32),
            jax.ShapeDtypeStruct((1, 128), F32),
        ),
        in_specs=[pl.BlockSpec(memory_space=pl.ANY)] * 7,
        out_specs=(
            pl.BlockSpec(memory_space=pl.ANY),
            pl.BlockSpec(memory_space=vmem),
            pl.BlockSpec(memory_space=vmem),
            pl.BlockSpec(memory_space=vmem),
        ),
        scratch_shapes=[
            vmem((4, HALF, D), BF16),
            vmem((TOK, D), BF16),
            vmem((TOK, D), BF16),
            vmem((TOK // KC, D, KC), BF16),
            vmem((HALF, D), BF16),
            vmem((TOK, D), BF16),
            vmem((TOK, D), BF16),
            vmem((TOK // KC, D, KC), BF16),
            vmem((512, D), BF16),
            vmem((D, HALF), F32),
            vmem((8, HALF), F32),
            vmem((4 * D, HALF), BF16),
            vmem((D, HALF), BF16),
            vmem((8, HALF), F32),
            vmem((NS, 8, 128), F32),
            vmem((D, HALF), BF16),
            vmem((D, HALF), F32),
            vmem((D, KC), F32),
            vmem((D, KC), F32),
            vmem((NS, 2, 2 * D, 128), BF16),
            vmem((4, 4, 2 * D, 128), BF16),
            vmem((NS, 2 * D, 128), BF16),
            vmem((HALF, D), BF16),
            vmem((NS, 2 * D, 128), BF16),
            vmem((NS, 8, 128), F32),
            vmem((TOK, QB), F32),
            vmem((TOK, QB), F32),
            vmem((8, QB), F32),
            pltpu.SemaphoreType.DMA((N_SEM,)),
            pltpu.SemaphoreType.DMA((N_SEM,)),
            pltpu.SemaphoreType.DMA,
        ],
        compiler_params=pltpu.CompilerParams(
            collective_id=0, has_side_effects=True, vmem_limit_bytes=56 * 1024 * 1024
        ),
        cost_estimate=pl.CostEstimate(
            flops=17_000_000_000, bytes_accessed=8_000_000, transcendentals=30_000_000
        ),
    )(tq, tk, tv, proj, sq, sk, sv)
    return dq.astype(F32), dk, dv, loss


def solution(mesh):
    rows = P("section", "seq", None)
    return jax.shard_map(
        body,
        mesh=mesh,
        in_specs=(rows, rows, rows, P("section", None, None, None), rows, rows, rows),
        out_specs=(rows, rows, rows, P("section", "seq")),
        check_vma=False,
    )
```

```python
import functools
import math

import jax
import jax.numpy as jnp
from jax import lax
from jax.experimental import pallas as pl
from jax.experimental.pallas import tpu as pltpu
from jax.sharding import PartitionSpec as P

D = 128
NS = 16
TOK = 4096
HALF = TOK // 2
ROOT = 1.0 / math.sqrt(D)
SCALE2 = ROOT * math.log2(math.e)
FLOOR = -1e30
MESH = pl.DeviceIdType.MESH
F32 = jnp.float32
BF16 = jnp.bfloat16


def dot_nt(x, y):
    return lax.dot_general(x, y, (((1,), (1,)), ((), ())), preferred_element_type=F32)


def dot_nn(x, y):
    return lax.dot_general(x, y, (((1,), (0,)), ((), ())), preferred_element_type=F32)


KC = 1024
QB = 512


def fold(x, op):
    out = x[:8]
    for i in range(8, x.shape[0], 8):
        out = op(out, x[i : i + 8])
    return out


def position(group, half):
    lane = lax.broadcasted_iota(jnp.int32, (1, QB), 1)
    return group * (2 * QB) + half * 128 + lax.div(lane, 128) * 256 + lax.rem(lane, 128)


class Flash:
    def __init__(self, half, keys, values_t, top, kept=None):
        self.half, self.keys, self.values_t, self.top, self.kept = half, keys, values_t, top, kept

    def take(self, top, query, chunk, buf):
        span = slice(chunk * KC, (chunk + 1) * KC)
        scores = dot_nt(self.keys[span, :], query)
        buf[span, :] = scores
        return jnp.maximum(top, fold(scores, jnp.maximum))

    def take_last(self, top, query, chunk, buf):
        at = position(chunk, self.half)
        start = chunk * KC
        low, high = slice(start, start + 512), slice(start + 512, start + 1024)
        key_pos = start + lax.broadcasted_iota(jnp.int32, (512, 256), 0)
        scores = dot_nt(self.keys[low, :], query)
        far = dot_nt(self.keys[high, :], query[256:, :])
        near = jnp.where(key_pos <= at[:, :256], scores[:, :256], FLOOR)
        far = jnp.where(key_pos + 512 <= at[:, 256:], far, FLOOR)
        buf[low, :256] = near
        buf[low, 256:] = scores[:, 256:]
        buf[high, 256:] = far
        right = jnp.maximum(fold(scores[:, 256:], jnp.maximum), fold(far, jnp.maximum))
        return jnp.maximum(top, jnp.concatenate([fold(near, jnp.maximum), right], axis=1))

    def mix(self, state, peak, chunk, buf, group):
        total, acc = state
        weights = jnp.exp2((buf[chunk * KC : (chunk + 1) * KC, :] - peak) * SCALE2)
        total = total + fold(weights, jnp.add)
        weights = weights.astype(BF16)
        if self.kept is not None:
            self.kept[kept_at(group, chunk)] = weights
        return total, acc + dot_nn(self.values_t[chunk], weights)

    def mix_last(self, state, peak, chunk, buf, group):
        total, acc = state
        start = chunk * KC
        near = jnp.exp2((buf[start : start + 512, :] - peak) * SCALE2)
        far = jnp.exp2((buf[start + 512 : start + 1024, 256:] - peak[:, 256:]) * SCALE2)
        sums = fold(near, jnp.add)
        total = total + jnp.concatenate(
            [sums[:, :256], sums[:, 256:] + fold(far, jnp.add)], axis=1
        )
        near, far = near.astype(BF16), far.astype(BF16)
        if self.kept is not None:
            self.kept[kept_at(group, chunk), :512, :] = near
            self.kept[kept_at(group, chunk), 512:, 256:] = far
        near = dot_nn(self.values_t[chunk, :, :512], near)
        far = dot_nn(self.values_t[chunk, :, 512:], far)
        return total, acc + jnp.concatenate([near[:, :256], near[:, 256:] + far], axis=1)

    def step(self, task, old, following, new):
        peak = top = None
        state = (jnp.zeros((8, QB), F32), jnp.zeros((D, QB), F32))
        mixes, takes = [], []
        if task is not None:
            peak = jnp.max(self.top[...], axis=0, keepdims=True)
            mixes = list(range(task[0] + 1))
        if following is not None:
            query = following[1]()
            top = jnp.full((8, QB), FLOOR, F32)
            takes = list(range(following[0] + 1))
        for chunk in range(max(len(mixes), len(takes))):
            if chunk < len(takes):
                step = self.take_last if chunk == following[0] else self.take
                top = step(top, query, chunk, new)
            if chunk < len(mixes):
                step = self.mix_last if chunk == task[0] else self.mix
                state = step(state, peak, chunk, old, task[0])
        if following is not None:
            self.top[...] = top
        if task is not None:
            task[2](peak, jnp.sum(state[0], axis=0, keepdims=True), state[1])


def kept_at(group, chunk):
    if isinstance(group, int):
        return group * (group + 1) // 2 + chunk
    return lax.div(group * (group + 1), 2) + chunk


def columns(group):
    if isinstance(group, int):
        return slice(group * QB, (group + 1) * QB)
    return pl.ds(pl.multiple_of(group * QB, QB), QB)


def student_forward(half, sq, sk, svt, ctx_t, scale, kept, work):
    score, top = work
    flash = Flash(half, sk, svt, top, kept)

    def task(group):
        at = columns(group)

        def finish(peak, total, acc):
            ctx_t[:, at] = acc / total
            scale[:, at] = jnp.broadcast_to(1.0 / total, (8, QB))

        return group, lambda: sq[at, :], finish

    tasks = [task(group) for group in (3, 2, 1, 0)]
    flash.step(None, None, tasks[0], score[0])
    for k in range(4):
        following = tasks[k + 1] if k < 3 else None
        flash.step(tasks[k], score[k % 2], following, score[(k + 1) % 2])


def teacher_forward(half, tq, tk, tvt, tctx_t, work, ready):
    score, top = work
    flash = Flash(half, tk, tvt, top)

    def task(head, group):
        at = columns(group)

        def finish(peak, total, acc):
            row = pl.multiple_of(head * D, D)
            tctx_t[pl.ds(row, D), at] = (acc / total).astype(BF16)

        return group, lambda: tq[head, at, :], finish

    ready(0)
    flash.step(None, None, task(0, 3), score[0])

    def pair(i, _):
        tasks = [task(2 * i, group) for group in (3, 2, 1, 0)]
        tasks += [task(2 * i + 1, group) for group in (0, 1, 2, 3)]
        for k in range(7):
            if k == 3:
                ready(2 * i + 1)
            flash.step(tasks[k], score[k % 2], tasks[k + 1], score[(k + 1) % 2])

        @pl.when(i == 0)
        def _():
            ready(2)
            flash.step(tasks[7], score[1], task(2, 3), score[0])

        @pl.when(i == 1)
        def _():
            flash.step(tasks[7], score[1], None, None)

        return 0

    lax.fori_loop(0, 2, pair, 0)


def turn_values(values, values_t):
    def chunk(i, _):
        values_t[i] = jnp.transpose(values[pl.ds(pl.multiple_of(i * KC, KC), KC), :])
        return 0

    lax.fori_loop(0, TOK // KC, chunk, 0)


def mismatches(tctx_t, proj, ctx_t, scale, grad_t, delta, loss):
    proj_t = jnp.transpose(proj[...])

    def step(group, _):
        at = columns(group)
        target = dot_nn(proj_t, tctx_t[:, at]).astype(BF16).astype(F32)
        context = ctx_t[:, at]
        miss = context - target
        per_total = scale[0:1, at]
        grad_t[:, at] = (miss * per_total).astype(BF16)
        dots = jnp.sum(fold(miss * context, jnp.add), axis=0, keepdims=True)
        delta[:, at] = jnp.broadcast_to(dots * per_total, (8, QB))
        squares = jnp.sum(fold(miss * miss, jnp.add), axis=0, keepdims=True) * (1.0 / 2048.0)
        wide = jnp.broadcast_to(squares, (8, QB))
        for i in range(4):
            loss[group * 4 + i] = wide[:, i * 128 : (i + 1) * 128]
        return 0

    lax.fori_loop(0, HALF // QB, step, 0)


def backward(first, sq, sk, sv, grad_t, kept, delta, q_t, dq_t, dk, dv, dkv, dq, middle, after, send_dq):
    dq_t[...] = jnp.zeros(dq_t.shape, F32)

    def outer(step, _):
        jb = lax.rem(first + step, TOK // KC)
        start = pl.multiple_of(jb * KC, KC)
        spans = [pl.ds(pl.multiple_of(start + e * 512, 512), 512) for e in range(2)]
        turned = [jnp.transpose(sk[span, :]) for span in spans]
        dk[...] = jnp.zeros(dk.shape, F32)
        dv[...] = jnp.zeros(dv.shape, F32)

        def terms(e, group, late=False):
            at, rows = columns(group), slice(e * 512, (e + 1) * 512)
            weights = kept.at[kept_at(group, jb)]
            if late:
                at = pl.ds(pl.multiple_of(group * QB + 256, 256), 256)
                prob = weights[rows, 256:]
            else:
                prob = weights[rows, :]
            query_t, grad = q_t[:, at], grad_t[:, at]
            ds = prob.astype(F32) * (dot_nn(sv[spans[e], :], grad) - delta[0:1, at])
            ds = ds.astype(BF16)
            dv[:, rows] += dot_nt(grad, prob)
            dk[:, rows] += dot_nt(query_t, ds)
            dq_t[:, at] += dot_nn(turned[e], ds)

        terms(0, jb)
        terms(1, jb, True)

        def leave(group):
            at = columns(group)
            dq[at, :] = (jnp.transpose(dq_t[:, at]) * ROOT).astype(BF16)
            send_dq(group)

        middle(step)

        @pl.when(jnp.logical_or(step + first >= TOK // KC, jnp.logical_and(first == 0, step >= 0)))
        def _():
            leave(jb)

        def full(group, _):
            terms(0, group)
            terms(1, group)

            @pl.when(jnp.logical_and(step == TOK // KC - 1, first > 0))
            def _():
                leave(group)

            return 0

        lax.fori_loop(jb + 1, HALF // QB, full, 0)
        for i in range(KC // 128):
            span = slice(i * 128, (i + 1) * 128)
            dkv[jb * 4 + i // 2, i % 2, :D, :] = (dk[:, span] * ROOT).astype(BF16)
            dkv[jb * 4 + i // 2, i % 2, D:, :] = dv[:, span].astype(BF16)
        after(step, jb)
        return 0

    lax.fori_loop(0, TOK // KC, outer, 0)


class Place:
    def __init__(self):
        self.section = lax.axis_index("section")
        self.s = lax.axis_index("seq")
        self.c = lax.rem(self.section, 2)
        self.base = self.section - self.c
        self.half = lax.rem(self.s, 2)
        self.h8 = head_of(self.s)
        self.head = self.c * 8 + self.h8
        self.me = self.c * NS + self.s


def head_of(s):
    return lax.rem(lax.div(s, 2), 4) * 2 + lax.div(s, 8)


def push(here, src, dst, send, recv, c, s):
    same = jnp.logical_and(c == here.c, s == here.s)

    @pl.when(same)
    def _():
        pltpu.make_async_copy(src, dst, recv).start()

    @pl.when(jnp.logical_not(same))
    def _():
        pltpu.make_async_remote_copy(
            src_ref=src, dst_ref=dst, send_sem=send, recv_sem=recv,
            device_id={"section": here.base + c, "seq": s}, device_id_type=MESH,
        ).start()


def toward(here, tx, tz):
    at = lax.div(here.s, 2)
    x = lax.rem(lax.div(at, 4) + tx, 2)
    z = lax.rem(lax.rem(at, 4) + jnp.where(here.half == 0, tz, 4 - tz), 4)
    return x * 4 + z


def greet(here):
    barrier = pltpu.get_barrier_semaphore()

    def signal(t, _):
        other = lax.rem(here.me + t, 2 * NS)
        pl.semaphore_signal(
            barrier, inc=1,
            device_id={"section": here.base + lax.div(other, NS), "seq": lax.rem(other, NS)},
            device_id_type=MESH,
        )
        return 0

    lax.fori_loop(1, 2 * NS, signal, 0)
    pl.semaphore_wait(barrier, 2 * NS - 1)


def drain(ref, sem):
    pltpu.make_async_copy(ref, ref, sem).wait()


S_K, S_V, S_Q, T_K, T_V, T_Q, G_Q, G_KV, LOSS = 0, 1, 2, 3, 4, 5, 9, 10, 11
FWD = 12
PAIR = 16
N_SEM = 20


def send_student(here, sq, sk, sv, sqb, skb, svb, send, recv):
    def step(t, _):
        c, p = lax.rem(here.c + lax.rem(t, 2), 2), toward(here, lax.rem(lax.div(t, 2), 2), lax.div(t, 4))
        h8 = head_of(2 * p)
        kv = pl.multiple_of((2 * c + lax.div(h8, 4)) * D, D)
        q = pl.multiple_of((c * 8 + h8) * D, D)
        at = pl.multiple_of(here.s * 256 + here.c * 128, 128)
        push(here, sk.at[0, :, pl.ds(kv, D)], skb.at[pl.ds(at, 128), :],
             send.at[S_K], recv.at[S_K], c, 2 * p)
        push(here, sv.at[0, :, pl.ds(kv, D)], svb.at[pl.ds(at, 128), :],
             send.at[S_V], recv.at[S_V], c, 2 * p + 1)
        to = pl.multiple_of(here.s * 128, 128)
        push(here, sq.at[0, :, pl.ds(q, D)], sqb.at[pl.ds(to, 128), :],
             send.at[S_Q], recv.at[S_Q], c, 2 * p + here.c)
        return 0

    lax.fori_loop(0, 16, step, 0)


def send_teacher(here, tq, tk, tv, tqb, tkb, tvb, send, recv):
    def step(t, _):
        p = toward(here, lax.rem(t, 2), lax.div(t, 2))
        kv = pl.multiple_of(lax.div(head_of(2 * p), 2) * D, D)
        at = pl.multiple_of(here.s * 256, 256)
        push(here, tk.at[0, :, pl.ds(kv, D)], tkb.at[pl.ds(at, 256), :],
             send.at[T_K], recv.at[T_K], here.c, 2 * p)
        push(here, tv.at[0, :, pl.ds(kv, D)], tvb.at[pl.ds(at, 256), :],
             send.at[T_V], recv.at[T_V], here.c, 2 * p + 1)
        return 0

    lax.fori_loop(0, 8, step, 0)
    for h in range(4):
        def query(t, _):
            p = toward(here, lax.rem(t, 2), lax.div(t, 2))
            col = pl.multiple_of(head_of(2 * p) * 512 + h * D, D)
            for core in range(2):
                push(here, tq.at[0, pl.ds(core * 128, 128), pl.ds(col, D)],
                     tqb.at[h, pl.ds(pl.multiple_of(here.s * 128, 128), 128), :],
                     send.at[T_Q + h], recv.at[T_Q + h], here.c, 2 * p + core)
            return 0

        lax.fori_loop(0, 8, query, 0)


def sibling(here, src, dst, send, recv):
    return pltpu.make_async_remote_copy(
        src_ref=src, dst_ref=dst, send_sem=send, recv_sem=recv,
        device_id={"section": here.section, "seq": here.s + 1 - 2 * here.half},
        device_id_type=MESH,
    )


def share(here, kb, vb, send, recv, k, v, fk, fv):
    @pl.when(here.half == 0)
    def _():
        drain(kb, recv.at[k])
        sibling(here, kb, kb, send.at[fk], recv.at[fk]).start()
        drain(vb, recv.at[fv])

    @pl.when(here.half == 1)
    def _():
        drain(vb, recv.at[v])
        sibling(here, vb, vb, send.at[fv], recv.at[fv]).start()
        drain(kb, recv.at[fk])


def kernel(tq, tk, tv, proj, sq, sk, sv, out_q, out_k, out_v, out_loss,
           tqb, tkb, tvb, tvt, sqb, skb, svb, svt, projb, ctx_t, scale, tctx_t, grad_t, delta, loss,
           kept, q_t, dq_t, dk, dv, dkv, paired, summed, dq, got_kv, got_loss,
           score0, score1, top, send, recv, local):
    here = Place()
    work = ((score0, score1), top)
    own_proj = pltpu.make_async_copy(proj.at[0, here.h8], projb, local)
    own_proj.start()
    greet(here)
    send_student(here, sq, sk, sv, sqb, skb, svb, send, recv)
    send_teacher(here, tq, tk, tv, tqb, tkb, tvb, send, recv)
    share(here, skb, svb, send, recv, S_K, S_V, FWD, FWD + 1)
    turn_values(svb, svt)
    drain(sqb, recv.at[S_Q])
    q_t[...] = jnp.transpose(sqb[...])
    student_forward(here.half, sqb, skb, svt, ctx_t, scale, kept, work)
    share(here, tkb, tvb, send, recv, T_K, T_V, FWD + 2, FWD + 3)
    turn_values(tvb, tvt)

    def ready(head):
        drain(tqb.at[head], recv.at[T_Q + head])

    teacher_forward(here.half, tqb, tkb, tvt, tctx_t, work, ready)
    own_proj.wait()
    mismatches(tctx_t, projb, ctx_t, scale, grad_t, delta, loss)

    def send_loss(t, _):
        s = lax.rem(here.s + t, NS)
        push(here, loss.at[s], got_loss.at[here.head], send.at[LOSS], recv.at[LOSS], here.half, s)
        return 0

    lax.fori_loop(0, NS, send_loss, 0)
    first = lax.rem(lax.div(here.s, 2), 4)

    def finish_kv(step):
        jb = lax.rem(first + step, 4)
        drain(paired.at[step], recv.at[PAIR + step])

        def one(i, _):
            s = jb * 4 + i
            mine = dkv[s, here.half].astype(F32) + paired[step, i].astype(F32)
            summed[s] = mine.astype(BF16)
            push(here, summed.at[s], got_kv.at[here.head], send.at[G_KV], recv.at[G_KV],
                 here.half, s)
            return 0

        lax.fori_loop(0, 4, one, 0)

    def after(step, jb):
        sibling(here, dkv.at[pl.ds(jb * 4, 4), 1 - here.half], paired.at[step],
                send.at[PAIR], recv.at[PAIR + step]).start()

    def middle(step):
        @pl.when(step > 0)
        def _():
            finish_kv(step - 1)

    def send_dq(group):
        def one(i, _):
            s = group * 4 + i
            row = pl.multiple_of(s * 128, 128)
            col = pl.multiple_of(here.head * D, D)
            push(here, dq.at[pl.ds(row, 128), :], out_q.at[0, :, pl.ds(col, D)],
                 send.at[G_Q], recv.at[G_Q], here.half, s)
            return 0

        lax.fori_loop(0, 4, one, 0)

    backward(first, sqb, skb, svb, grad_t, kept, delta, q_t, dq_t, dk, dv, dkv, dq,
             middle, after, send_dq)
    finish_kv(3)

    drain(got_loss, recv.at[LOSS])
    sums = got_loss[0]
    for h in range(1, 16):
        sums = sums + got_loss[h]
    out_loss[...] = sums[0:1, :]
    drain(got_kv, recv.at[G_KV])
    for g in range(4):
        sums = got_kv[g * 4].astype(F32)
        for i in range(1, 4):
            sums = sums + got_kv[g * 4 + i].astype(F32)
        out_k[0, :, g * D : (g + 1) * D] = jnp.transpose(sums[:D])
        out_v[0, :, g * D : (g + 1) * D] = jnp.transpose(sums[D:])
    drain(out_q, recv.at[G_Q])

    own_core = here.half == 0

    @pl.when(own_core)
    def _():
        drain(skb.at[pl.ds(0, 15 * 128), :], send.at[S_K])
        drain(svb.at[pl.ds(0, 16 * 128), :], send.at[S_V])
        drain(tkb.at[pl.ds(0, 7 * 256), :], send.at[T_K])
        drain(tvb.at[pl.ds(0, 8 * 256), :], send.at[T_V])
        drain(skb, send.at[FWD])
        drain(tkb, send.at[FWD + 2])

    @pl.when(jnp.logical_not(own_core))
    def _():
        drain(skb.at[pl.ds(0, 16 * 128), :], send.at[S_K])
        drain(svb.at[pl.ds(0, 15 * 128), :], send.at[S_V])
        drain(tkb.at[pl.ds(0, 8 * 256), :], send.at[T_K])
        drain(tvb.at[pl.ds(0, 7 * 256), :], send.at[T_V])
        drain(svb, send.at[FWD + 1])
        drain(tvb, send.at[FWD + 3])

    for h in range(4):
        drain(tqb.at[h, pl.ds(0, 15 * 128), :], send.at[T_Q + h])
    drain(paired, send.at[PAIR])
    with_self = here.half == here.c

    @pl.when(with_self)
    def _():
        drain(sqb.at[pl.ds(0, 15 * 128), :], send.at[S_Q])
        drain(dq.at[pl.ds(0, 15 * 128), :], send.at[G_Q])
        drain(loss.at[pl.ds(0, 15)], send.at[LOSS])
        drain(got_kv.at[pl.ds(0, 15)], send.at[G_KV])

    @pl.when(jnp.logical_not(with_self))
    def _():
        drain(sqb, send.at[S_Q])
        drain(dq, send.at[G_Q])
        drain(loss, send.at[LOSS])
        drain(got_kv, send.at[G_KV])


def body(tq, tk, tv, proj, sq, sk, sv):
    vmem = pltpu.VMEM
    dq, dk, dv, loss = pl.pallas_call(
        kernel,
        out_shape=(
            jax.ShapeDtypeStruct((1, 128, 2048), BF16),
            jax.ShapeDtypeStruct((1, 128, 512), F32),
            jax.ShapeDtypeStruct((1, 128, 512), F32),
            jax.ShapeDtypeStruct((1, 128), F32),
        ),
        in_specs=[pl.BlockSpec(memory_space=pl.ANY)] * 7,
        out_specs=(
            pl.BlockSpec(memory_space=pl.ANY),
            pl.BlockSpec(memory_space=vmem),
            pl.BlockSpec(memory_space=vmem),
            pl.BlockSpec(memory_space=vmem),
        ),
        scratch_shapes=[
            vmem((4, HALF, D), BF16),
            vmem((TOK, D), BF16),
            vmem((TOK, D), BF16),
            vmem((TOK // KC, D, KC), BF16),
            vmem((HALF, D), BF16),
            vmem((TOK, D), BF16),
            vmem((TOK, D), BF16),
            vmem((TOK // KC, D, KC), BF16),
            vmem((512, D), BF16),
            vmem((D, HALF), F32),
            vmem((8, HALF), F32),
            vmem((4 * D, HALF), BF16),
            vmem((D, HALF), BF16),
            vmem((8, HALF), F32),
            vmem((NS, 8, 128), F32),
            vmem((10, KC, QB), BF16),
            vmem((D, HALF), BF16),
            vmem((D, HALF), F32),
            vmem((D, KC), F32),
            vmem((D, KC), F32),
            vmem((NS, 2, 2 * D, 128), BF16),
            vmem((4, 4, 2 * D, 128), BF16),
            vmem((NS, 2 * D, 128), BF16),
            vmem((HALF, D), BF16),
            vmem((NS, 2 * D, 128), BF16),
            vmem((NS, 8, 128), F32),
            vmem((TOK, QB), F32),
            vmem((TOK, QB), F32),
            vmem((8, QB), F32),
            pltpu.SemaphoreType.DMA((N_SEM,)),
            pltpu.SemaphoreType.DMA((N_SEM,)),
            pltpu.SemaphoreType.DMA,
        ],
        compiler_params=pltpu.CompilerParams(
            collective_id=0, has_side_effects=True, vmem_limit_bytes=60 * 1024 * 1024
        ),
        cost_estimate=pl.CostEstimate(
            flops=17_000_000_000, bytes_accessed=8_000_000, transcendentals=30_000_000
        ),
    )(tq, tk, tv, proj, sq, sk, sv)
    return dq.astype(F32), dk, dv, loss


def solution(mesh):
    rows = P("section", "seq", None)
    return jax.shard_map(
        body,
        mesh=mesh,
        in_specs=(rows, rows, rows, P("section", None, None, None), rows, rows, rows),
        out_specs=(rows, rows, rows, P("section", "seq")),
        check_vma=False,
    )
```

```python
import functools
import math

import jax
import jax.numpy as jnp
from jax import lax
from jax.experimental import pallas as pl
from jax.experimental.pallas import tpu as pltpu
from jax.sharding import PartitionSpec as P

D = 128
NS = 16
TOK = 4096
HALF = TOK // 2
ROOT = 1.0 / math.sqrt(D)
SCALE2 = ROOT * math.log2(math.e)
FLOOR = -1e30
MESH = pl.DeviceIdType.MESH
F32 = jnp.float32
BF16 = jnp.bfloat16


def dot_nt(x, y):
    return lax.dot_general(x, y, (((1,), (1,)), ((), ())), preferred_element_type=F32)


def dot_nn(x, y):
    return lax.dot_general(x, y, (((1,), (0,)), ((), ())), preferred_element_type=F32)


KC = 1024
QB = 512


def fold(x, op):
    out = x[:8]
    for i in range(8, x.shape[0], 8):
        out = op(out, x[i : i + 8])
    return out


def position(group, half):
    lane = lax.broadcasted_iota(jnp.int32, (1, QB), 1)
    return group * (2 * QB) + half * 128 + lax.div(lane, 128) * 256 + lax.rem(lane, 128)


class Flash:
    def __init__(self, half, keys, values_t, top, kept=None):
        self.half, self.keys, self.values_t, self.top, self.kept = half, keys, values_t, top, kept

    def take(self, top, query, chunk, buf):
        span = slice(chunk * KC, (chunk + 1) * KC)
        scores = dot_nt(self.keys[span, :], query)
        buf[span, :] = scores
        return jnp.maximum(top, fold(scores, jnp.maximum))

    def take_last(self, top, query, chunk, buf):
        at = position(chunk, self.half)
        start = chunk * KC
        low, high = slice(start, start + 512), slice(start + 512, start + 1024)
        key_pos = start + lax.broadcasted_iota(jnp.int32, (512, 256), 0)
        scores = dot_nt(self.keys[low, :], query)
        far = dot_nt(self.keys[high, :], query[256:, :])
        near = jnp.where(key_pos <= at[:, :256], scores[:, :256], FLOOR)
        far = jnp.where(key_pos + 512 <= at[:, 256:], far, FLOOR)
        buf[low, :256] = near
        buf[low, 256:] = scores[:, 256:]
        buf[high, 256:] = far
        right = jnp.maximum(fold(scores[:, 256:], jnp.maximum), fold(far, jnp.maximum))
        return jnp.maximum(top, jnp.concatenate([fold(near, jnp.maximum), right], axis=1))

    def mix(self, state, peak, chunk, buf, group):
        total, acc = state
        weights = jnp.exp2((buf[chunk * KC : (chunk + 1) * KC, :] - peak) * SCALE2)
        total = total + fold(weights, jnp.add)
        weights = weights.astype(BF16)
        if self.kept is not None:
            self.kept[kept_at(group, chunk)] = weights
        return total, acc + dot_nn(self.values_t[chunk], weights)

    def mix_last(self, state, peak, chunk, buf, group):
        total, acc = state
        start = chunk * KC
        near = jnp.exp2((buf[start : start + 512, :] - peak) * SCALE2)
        far = jnp.exp2((buf[start + 512 : start + 1024, 256:] - peak[:, 256:]) * SCALE2)
        sums = fold(near, jnp.add)
        total = total + jnp.concatenate(
            [sums[:, :256], sums[:, 256:] + fold(far, jnp.add)], axis=1
        )
        near, far = near.astype(BF16), far.astype(BF16)
        if self.kept is not None:
            self.kept[kept_at(group, chunk), :512, :] = near
            self.kept[kept_at(group, chunk), 512:, 256:] = far
        near = dot_nn(self.values_t[chunk, :, :512], near)
        far = dot_nn(self.values_t[chunk, :, 512:], far)
        return total, acc + jnp.concatenate([near[:, :256], near[:, 256:] + far], axis=1)

    def step(self, task, old, following, new):
        peak = top = None
        state = (jnp.zeros((8, QB), F32), jnp.zeros((D, QB), F32))
        mixes, takes = [], []
        if task is not None:
            peak = jnp.max(self.top[...], axis=0, keepdims=True)
            mixes = list(range(task[0] + 1))
        if following is not None:
            query = following[1]()
            top = jnp.full((8, QB), FLOOR, F32)
            takes = list(range(following[0] + 1))
        for chunk in range(max(len(mixes), len(takes))):
            if chunk < len(takes):
                step = self.take_last if chunk == following[0] else self.take
                top = step(top, query, chunk, new)
            if chunk < len(mixes):
                step = self.mix_last if chunk == task[0] else self.mix
                state = step(state, peak, chunk, old, task[0])
        if following is not None:
            self.top[...] = top
        if task is not None:
            task[2](peak, jnp.sum(state[0], axis=0, keepdims=True), state[1])


def kept_at(group, chunk):
    if isinstance(group, int):
        return group * (group + 1) // 2 + chunk
    return lax.div(group * (group + 1), 2) + chunk


def columns(group):
    if isinstance(group, int):
        return slice(group * QB, (group + 1) * QB)
    return pl.ds(pl.multiple_of(group * QB, QB), QB)


def student_forward(half, sq, sk, svt, ctx_t, scale, kept, work):
    score, top = work
    flash = Flash(half, sk, svt, top, kept)

    def task(group):
        at = columns(group)

        def finish(peak, total, acc):
            ctx_t[:, at] = acc / total
            scale[:, at] = jnp.broadcast_to(1.0 / total, (8, QB))

        return group, lambda: sq[at, :], finish

    tasks = [task(group) for group in (3, 2, 1, 0)]
    flash.step(None, None, tasks[0], score[0])
    for k in range(4):
        following = tasks[k + 1] if k < 3 else None
        flash.step(tasks[k], score[k % 2], following, score[(k + 1) % 2])


def teacher_forward(half, tq, tk, tvt, tctx_t, work, ready):
    score, top = work
    flash = Flash(half, tk, tvt, top)

    def task(head, group):
        at = columns(group)

        def finish(peak, total, acc):
            row = pl.multiple_of(head * D, D)
            tctx_t[pl.ds(row, D), at] = (acc / total).astype(BF16)

        return group, lambda: tq[head, at, :], finish

    ready(0)
    flash.step(None, None, task(0, 3), score[0])

    def pair(i, _):
        tasks = [task(2 * i, group) for group in (3, 2, 1, 0)]
        tasks += [task(2 * i + 1, group) for group in (0, 1, 2, 3)]
        for k in range(7):
            if k == 3:
                ready(2 * i + 1)
            flash.step(tasks[k], score[k % 2], tasks[k + 1], score[(k + 1) % 2])

        @pl.when(i == 0)
        def _():
            ready(2)
            flash.step(tasks[7], score[1], task(2, 3), score[0])

        @pl.when(i == 1)
        def _():
            flash.step(tasks[7], score[1], None, None)

        return 0

    lax.fori_loop(0, 2, pair, 0)


def turn_values(values, values_t):
    def chunk(i, _):
        values_t[i] = jnp.transpose(values[pl.ds(pl.multiple_of(i * KC, KC), KC), :])
        return 0

    lax.fori_loop(0, TOK // KC, chunk, 0)


def mismatches(tctx_t, proj, ctx_t, scale, grad_t, delta, loss):
    proj_t = jnp.transpose(proj[...])

    def step(group, _):
        at = columns(group)
        target = dot_nn(proj_t, tctx_t[:, at]).astype(BF16).astype(F32)
        context = ctx_t[:, at]
        miss = context - target
        per_total = scale[0:1, at]
        grad_t[:, at] = (miss * per_total).astype(BF16)
        dots = jnp.sum(fold(miss * context, jnp.add), axis=0, keepdims=True)
        delta[:, at] = jnp.broadcast_to(dots * per_total, (8, QB))
        squares = jnp.sum(fold(miss * miss, jnp.add), axis=0, keepdims=True) * (1.0 / 2048.0)
        wide = jnp.broadcast_to(squares, (8, QB))
        for i in range(4):
            loss[group * 4 + i] = wide[:, i * 128 : (i + 1) * 128]
        return 0

    lax.fori_loop(0, HALF // QB, step, 0)


def backward(first, sq, sk, sv, grad_t, kept, delta, q_t, dq_t, dk, dv, dkv, dq, middle, after, send_dq, spin):
    dq_t[...] = jnp.zeros(dq_t.shape, F32)

    def outer(step, _):
        jb = lax.rem(first + step, TOK // KC)
        start = pl.multiple_of(jb * KC, KC)
        spans = [pl.ds(pl.multiple_of(start + e * 512, 512), 512) for e in range(2)]
        turned = [jnp.transpose(sk[span, :]) for span in spans]
        dk[...] = jnp.zeros(dk.shape, F32)
        dv[...] = jnp.zeros(dv.shape, F32)

        def terms(e, group, late=False):
            at, rows = columns(group), slice(e * 512, (e + 1) * 512)
            weights = kept.at[kept_at(group, jb)]
            if late:
                at = pl.ds(pl.multiple_of(group * QB + 256, 256), 256)
                prob = weights[rows, 256:]
            else:
                prob = weights[rows, :]
            query_t, grad = q_t[:, at], grad_t[:, at]
            ds = prob.astype(F32) * (dot_nn(sv[spans[e], :], grad) - delta[0:1, at])
            ds = ds.astype(BF16)
            dv[:, rows] += dot_nt(grad, prob)
            dk[:, rows] += dot_nt(query_t, ds)
            dq_t[:, at] += dot_nn(turned[e], ds)

        terms(0, jb)
        terms(1, jb, True)

        def leave(group):
            at = columns(group)
            dq[at, :] = (jnp.transpose(dq_t[:, at]) * ROOT).astype(BF16)
            send_dq(group)

        middle(step)

        @pl.when(jnp.logical_or(step + first >= TOK // KC, jnp.logical_and(first == 0, step >= 0)))
        def _():
            leave(jb)

        left = HALF // QB - 1 - jb

        def full(turn, _):
            group = jb + 1 + lax.rem(turn + spin, left)
            terms(0, group)
            terms(1, group)

            @pl.when(jnp.logical_and(step == TOK // KC - 1, first > 0))
            def _():
                leave(group)

            return 0

        lax.fori_loop(0, left, full, 0)
        for i in range(KC // 128):
            span = slice(i * 128, (i + 1) * 128)
            dkv[jb * 4 + i // 2, i % 2, :D, :] = (dk[:, span] * ROOT).astype(BF16)
            dkv[jb * 4 + i // 2, i % 2, D:, :] = dv[:, span].astype(BF16)
        after(step, jb)
        return 0

    lax.fori_loop(0, TOK // KC, outer, 0)


class Place:
    def __init__(self):
        self.section = lax.axis_index("section")
        self.s = lax.axis_index("seq")
        self.c = lax.rem(self.section, 2)
        self.base = self.section - self.c
        self.half = lax.rem(self.s, 2)
        self.h8 = head_of(self.s)
        self.head = self.c * 8 + self.h8
        self.me = self.c * NS + self.s


def head_of(s):
    return lax.rem(lax.div(s, 2), 4) * 2 + lax.div(s, 8)


def push(here, src, dst, send, recv, c, s):
    same = jnp.logical_and(c == here.c, s == here.s)

    @pl.when(same)
    def _():
        pltpu.make_async_copy(src, dst, recv).start()

    @pl.when(jnp.logical_not(same))
    def _():
        pltpu.make_async_remote_copy(
            src_ref=src, dst_ref=dst, send_sem=send, recv_sem=recv,
            device_id={"section": here.base + c, "seq": s}, device_id_type=MESH,
        ).start()


def toward(here, tx, tz):
    at = lax.div(here.s, 2)
    x = lax.rem(lax.div(at, 4) + tx, 2)
    z = lax.rem(lax.rem(at, 4) + jnp.where(here.half == 0, tz, 4 - tz), 4)
    return x * 4 + z


def greet(here):
    barrier = pltpu.get_barrier_semaphore()

    def signal(t, _):
        other = lax.rem(here.me + t, 2 * NS)
        pl.semaphore_signal(
            barrier, inc=1,
            device_id={"section": here.base + lax.div(other, NS), "seq": lax.rem(other, NS)},
            device_id_type=MESH,
        )
        return 0

    lax.fori_loop(1, 2 * NS, signal, 0)
    pl.semaphore_wait(barrier, 2 * NS - 1)


def drain(ref, sem):
    pltpu.make_async_copy(ref, ref, sem).wait()


S_K, S_V, S_Q, T_K, T_V, T_Q, G_Q, G_KV, LOSS = 0, 1, 2, 3, 4, 5, 9, 10, 11
FWD = 12
PAIR = 16
N_SEM = 20


def send_student(here, sq, sk, sv, sqb, skb, svb, send, recv):
    def step(t, _):
        c, p = lax.rem(here.c + lax.rem(t, 2), 2), toward(here, lax.rem(lax.div(t, 2), 2), lax.div(t, 4))
        h8 = head_of(2 * p)
        kv = pl.multiple_of((2 * c + lax.div(h8, 4)) * D, D)
        q = pl.multiple_of((c * 8 + h8) * D, D)
        at = pl.multiple_of(here.s * 256 + here.c * 128, 128)
        push(here, sk.at[0, :, pl.ds(kv, D)], skb.at[pl.ds(at, 128), :],
             send.at[S_K], recv.at[S_K], c, 2 * p)
        push(here, sv.at[0, :, pl.ds(kv, D)], svb.at[pl.ds(at, 128), :],
             send.at[S_V], recv.at[S_V], c, 2 * p + 1)
        to = pl.multiple_of(here.s * 128, 128)
        push(here, sq.at[0, :, pl.ds(q, D)], sqb.at[pl.ds(to, 128), :],
             send.at[S_Q], recv.at[S_Q], c, 2 * p + here.c)
        return 0

    lax.fori_loop(0, 16, step, 0)


def send_teacher(here, tq, tk, tv, tqb, tkb, tvb, send, recv):
    def step(t, _):
        p = toward(here, lax.rem(t, 2), lax.div(t, 2))
        kv = pl.multiple_of(lax.div(head_of(2 * p), 2) * D, D)
        at = pl.multiple_of(here.s * 256, 256)
        push(here, tk.at[0, :, pl.ds(kv, D)], tkb.at[pl.ds(at, 256), :],
             send.at[T_K], recv.at[T_K], here.c, 2 * p)
        push(here, tv.at[0, :, pl.ds(kv, D)], tvb.at[pl.ds(at, 256), :],
             send.at[T_V], recv.at[T_V], here.c, 2 * p + 1)
        return 0

    lax.fori_loop(0, 8, step, 0)
    for h in range(4):
        def query(t, _):
            p = toward(here, lax.rem(t, 2), lax.div(t, 2))
            col = pl.multiple_of(head_of(2 * p) * 512 + h * D, D)
            for core in range(2):
                push(here, tq.at[0, pl.ds(core * 128, 128), pl.ds(col, D)],
                     tqb.at[h, pl.ds(pl.multiple_of(here.s * 128, 128), 128), :],
                     send.at[T_Q + h], recv.at[T_Q + h], here.c, 2 * p + core)
            return 0

        lax.fori_loop(0, 8, query, 0)


def sibling(here, src, dst, send, recv):
    return pltpu.make_async_remote_copy(
        src_ref=src, dst_ref=dst, send_sem=send, recv_sem=recv,
        device_id={"section": here.section, "seq": here.s + 1 - 2 * here.half},
        device_id_type=MESH,
    )


def share(here, kb, vb, send, recv, k, v, fk, fv):
    @pl.when(here.half == 0)
    def _():
        drain(kb, recv.at[k])
        sibling(here, kb, kb, send.at[fk], recv.at[fk]).start()
        drain(vb, recv.at[fv])

    @pl.when(here.half == 1)
    def _():
        drain(vb, recv.at[v])
        sibling(here, vb, vb, send.at[fv], recv.at[fv]).start()
        drain(kb, recv.at[fk])


def kernel(tq, tk, tv, proj, sq, sk, sv, out_q, out_k, out_v, out_loss,
           tqb, tkb, tvb, tvt, sqb, skb, svb, svt, projb, ctx_t, scale, tctx_t, grad_t, delta, loss,
           kept, q_t, dq_t, dk, dv, dkv, paired, summed, dq, got_kv, got_loss,
           score0, score1, top, send, recv, local):
    here = Place()
    work = ((score0, score1), top)
    own_proj = pltpu.make_async_copy(proj.at[0, here.h8], projb, local)
    own_proj.start()
    greet(here)
    send_student(here, sq, sk, sv, sqb, skb, svb, send, recv)
    send_teacher(here, tq, tk, tv, tqb, tkb, tvb, send, recv)
    share(here, skb, svb, send, recv, S_K, S_V, FWD, FWD + 1)
    turn_values(svb, svt)
    drain(sqb, recv.at[S_Q])
    q_t[...] = jnp.transpose(sqb[...])
    student_forward(here.half, sqb, skb, svt, ctx_t, scale, kept, work)
    share(here, tkb, tvb, send, recv, T_K, T_V, FWD + 2, FWD + 3)
    turn_values(tvb, tvt)

    def ready(head):
        drain(tqb.at[head], recv.at[T_Q + head])

    teacher_forward(here.half, tqb, tkb, tvt, tctx_t, work, ready)
    own_proj.wait()
    mismatches(tctx_t, projb, ctx_t, scale, grad_t, delta, loss)

    def send_loss(t, _):
        s = lax.rem(here.s + t, NS)
        push(here, loss.at[s], got_loss.at[here.head], send.at[LOSS], recv.at[LOSS], here.half, s)
        return 0

    lax.fori_loop(0, NS, send_loss, 0)
    z = lax.rem(lax.div(here.s, 2), 4)
    first = lax.rem(z + lax.div(here.s, 8) + 2 * here.c, 4)

    def finish_kv(step):
        jb = lax.rem(first + step, 4)
        drain(paired.at[step], recv.at[PAIR + step])

        def one(i, _):
            s = jb * 4 + i
            mine = dkv[s, here.half].astype(F32) + paired[step, i].astype(F32)
            summed[s] = mine.astype(BF16)
            push(here, summed.at[s], got_kv.at[here.head], send.at[G_KV], recv.at[G_KV],
                 here.half, s)
            return 0

        lax.fori_loop(0, 4, one, 0)

    def after(step, jb):
        sibling(here, dkv.at[pl.ds(jb * 4, 4), 1 - here.half], paired.at[step],
                send.at[PAIR], recv.at[PAIR + step]).start()

    def middle(step):
        @pl.when(step > 0)
        def _():
            finish_kv(step - 1)

    def send_dq(group):
        def one(i, _):
            s = group * 4 + i
            row = pl.multiple_of(s * 128, 128)
            col = pl.multiple_of(here.head * D, D)
            push(here, dq.at[pl.ds(row, 128), :], out_q.at[0, :, pl.ds(col, D)],
                 send.at[G_Q], recv.at[G_Q], here.half, s)
            return 0

        lax.fori_loop(0, 4, one, 0)

    backward(first, sqb, skb, svb, grad_t, kept, delta, q_t, dq_t, dk, dv, dkv, dq,
             middle, after, send_dq, z)
    finish_kv(3)

    drain(got_loss, recv.at[LOSS])
    sums = got_loss[0]
    for h in range(1, 16):
        sums = sums + got_loss[h]
    out_loss[...] = sums[0:1, :]
    drain(got_kv, recv.at[G_KV])
    for g in range(4):
        sums = got_kv[g * 4].astype(F32)
        for i in range(1, 4):
            sums = sums + got_kv[g * 4 + i].astype(F32)
        out_k[0, :, g * D : (g + 1) * D] = jnp.transpose(sums[:D])
        out_v[0, :, g * D : (g + 1) * D] = jnp.transpose(sums[D:])
    drain(out_q, recv.at[G_Q])

    own_core = here.half == 0

    @pl.when(own_core)
    def _():
        drain(skb.at[pl.ds(0, 15 * 128), :], send.at[S_K])
        drain(svb.at[pl.ds(0, 16 * 128), :], send.at[S_V])
        drain(tkb.at[pl.ds(0, 7 * 256), :], send.at[T_K])
        drain(tvb.at[pl.ds(0, 8 * 256), :], send.at[T_V])
        drain(skb, send.at[FWD])
        drain(tkb, send.at[FWD + 2])

    @pl.when(jnp.logical_not(own_core))
    def _():
        drain(skb.at[pl.ds(0, 16 * 128), :], send.at[S_K])
        drain(svb.at[pl.ds(0, 15 * 128), :], send.at[S_V])
        drain(tkb.at[pl.ds(0, 8 * 256), :], send.at[T_K])
        drain(tvb.at[pl.ds(0, 7 * 256), :], send.at[T_V])
        drain(svb, send.at[FWD + 1])
        drain(tvb, send.at[FWD + 3])

    for h in range(4):
        drain(tqb.at[h, pl.ds(0, 15 * 128), :], send.at[T_Q + h])
    drain(paired, send.at[PAIR])
    with_self = here.half == here.c

    @pl.when(with_self)
    def _():
        drain(sqb.at[pl.ds(0, 15 * 128), :], send.at[S_Q])
        drain(dq.at[pl.ds(0, 15 * 128), :], send.at[G_Q])
        drain(loss.at[pl.ds(0, 15)], send.at[LOSS])
        drain(got_kv.at[pl.ds(0, 15)], send.at[G_KV])

    @pl.when(jnp.logical_not(with_self))
    def _():
        drain(sqb, send.at[S_Q])
        drain(dq, send.at[G_Q])
        drain(loss, send.at[LOSS])
        drain(got_kv, send.at[G_KV])


def body(tq, tk, tv, proj, sq, sk, sv):
    vmem = pltpu.VMEM
    dq, dk, dv, loss = pl.pallas_call(
        kernel,
        out_shape=(
            jax.ShapeDtypeStruct((1, 128, 2048), BF16),
            jax.ShapeDtypeStruct((1, 128, 512), F32),
            jax.ShapeDtypeStruct((1, 128, 512), F32),
            jax.ShapeDtypeStruct((1, 128), F32),
        ),
        in_specs=[pl.BlockSpec(memory_space=pl.ANY)] * 7,
        out_specs=(
            pl.BlockSpec(memory_space=pl.ANY),
            pl.BlockSpec(memory_space=vmem),
            pl.BlockSpec(memory_space=vmem),
            pl.BlockSpec(memory_space=vmem),
        ),
        scratch_shapes=[
            vmem((4, HALF, D), BF16),
            vmem((TOK, D), BF16),
            vmem((TOK, D), BF16),
            vmem((TOK // KC, D, KC), BF16),
            vmem((HALF, D), BF16),
            vmem((TOK, D), BF16),
            vmem((TOK, D), BF16),
            vmem((TOK // KC, D, KC), BF16),
            vmem((512, D), BF16),
            vmem((D, HALF), F32),
            vmem((8, HALF), F32),
            vmem((4 * D, HALF), BF16),
            vmem((D, HALF), BF16),
            vmem((8, HALF), F32),
            vmem((NS, 8, 128), F32),
            vmem((10, KC, QB), BF16),
            vmem((D, HALF), BF16),
            vmem((D, HALF), F32),
            vmem((D, KC), F32),
            vmem((D, KC), F32),
            vmem((NS, 2, 2 * D, 128), BF16),
            vmem((4, 4, 2 * D, 128), BF16),
            vmem((NS, 2 * D, 128), BF16),
            vmem((HALF, D), BF16),
            vmem((NS, 2 * D, 128), BF16),
            vmem((NS, 8, 128), F32),
            vmem((TOK, QB), F32),
            vmem((TOK, QB), F32),
            vmem((8, QB), F32),
            pltpu.SemaphoreType.DMA((N_SEM,)),
            pltpu.SemaphoreType.DMA((N_SEM,)),
            pltpu.SemaphoreType.DMA,
        ],
        compiler_params=pltpu.CompilerParams(
            collective_id=0, has_side_effects=True, vmem_limit_bytes=60 * 1024 * 1024
        ),
        cost_estimate=pl.CostEstimate(
            flops=17_000_000_000, bytes_accessed=8_000_000, transcendentals=30_000_000
        ),
    )(tq, tk, tv, proj, sq, sk, sv)
    return dq.astype(F32), dk, dv, loss


def solution(mesh):
    rows = P("section", "seq", None)
    return jax.shard_map(
        body,
        mesh=mesh,
        in_specs=(rows, rows, rows, P("section", None, None, None), rows, rows, rows),
        out_specs=(rows, rows, rows, P("section", "seq")),
        check_vma=False,
    )
```

```python
import functools
import math

import jax
import jax.numpy as jnp
from jax import lax
from jax.experimental import pallas as pl
from jax.experimental.pallas import tpu as pltpu
from jax.sharding import PartitionSpec as P

D = 128
NS = 16
TOK = 4096
HALF = TOK // 2
ROOT = 1.0 / math.sqrt(D)
SCALE2 = ROOT * math.log2(math.e)
FLOOR = -1e30
MESH = pl.DeviceIdType.MESH
F32 = jnp.float32
BF16 = jnp.bfloat16


def dot_nt(x, y):
    return lax.dot_general(x, y, (((1,), (1,)), ((), ())), preferred_element_type=F32)


def dot_nn(x, y):
    return lax.dot_general(x, y, (((1,), (0,)), ((), ())), preferred_element_type=F32)


KC = 1024
QB = 512


def fold(x, op):
    out = x[:8]
    for i in range(8, x.shape[0], 8):
        out = op(out, x[i : i + 8])
    return out


def position(group, half):
    lane = lax.broadcasted_iota(jnp.int32, (1, QB), 1)
    return group * (2 * QB) + half * 128 + lax.div(lane, 128) * 256 + lax.rem(lane, 128)


class Flash:
    def __init__(self, half, keys, values_t, top, kept=None):
        self.half, self.keys, self.values_t, self.top, self.kept = half, keys, values_t, top, kept

    def take(self, top, query, chunk, buf):
        span = slice(chunk * KC, (chunk + 1) * KC)
        scores = dot_nt(self.keys[span, :], query)
        buf[span, :] = scores
        return jnp.maximum(top, fold(scores, jnp.maximum))

    def take_last(self, top, query, chunk, buf):
        at = position(chunk, self.half)
        start = chunk * KC
        low, high = slice(start, start + 512), slice(start + 512, start + 1024)
        key_pos = start + lax.broadcasted_iota(jnp.int32, (512, 256), 0)
        scores = dot_nt(self.keys[low, :], query)
        far = dot_nt(self.keys[high, :], query[256:, :])
        near = jnp.where(key_pos <= at[:, :256], scores[:, :256], FLOOR)
        far = jnp.where(key_pos + 512 <= at[:, 256:], far, FLOOR)
        buf[low, :256] = near
        buf[low, 256:] = scores[:, 256:]
        buf[high, 256:] = far
        right = jnp.maximum(fold(scores[:, 256:], jnp.maximum), fold(far, jnp.maximum))
        return jnp.maximum(top, jnp.concatenate([fold(near, jnp.maximum), right], axis=1))

    def mix(self, state, peak, chunk, buf, group):
        total, acc = state
        weights = jnp.exp2((buf[chunk * KC : (chunk + 1) * KC, :] - peak) * SCALE2)
        total = total + fold(weights, jnp.add)
        weights = weights.astype(BF16)
        if self.kept is not None:
            self.kept[kept_at(group, chunk)] = weights
        return total, acc + dot_nn(self.values_t[chunk], weights)

    def mix_last(self, state, peak, chunk, buf, group):
        total, acc = state
        start = chunk * KC
        near = jnp.exp2((buf[start : start + 512, :] - peak) * SCALE2)
        far = jnp.exp2((buf[start + 512 : start + 1024, 256:] - peak[:, 256:]) * SCALE2)
        sums = fold(near, jnp.add)
        total = total + jnp.concatenate(
            [sums[:, :256], sums[:, 256:] + fold(far, jnp.add)], axis=1
        )
        near, far = near.astype(BF16), far.astype(BF16)
        if self.kept is not None:
            self.kept[kept_at(group, chunk), :512, :] = near
            self.kept[kept_at(group, chunk), 512:, 256:] = far
        near = dot_nn(self.values_t[chunk, :, :512], near)
        far = dot_nn(self.values_t[chunk, :, 512:], far)
        return total, acc + jnp.concatenate([near[:, :256], near[:, 256:] + far], axis=1)

    def step(self, task, old, following, new):
        peak = top = None
        state = (jnp.zeros((8, QB), F32), jnp.zeros((D, QB), F32))
        mixes, takes = [], []
        if task is not None:
            peak = jnp.max(self.top[...], axis=0, keepdims=True)
            mixes = list(range(task[0] + 1))
        if following is not None:
            query = following[1]()
            top = jnp.full((8, QB), FLOOR, F32)
            takes = list(range(following[0] + 1))
        for chunk in range(max(len(mixes), len(takes))):
            if chunk < len(takes):
                step = self.take_last if chunk == following[0] else self.take
                top = step(top, query, chunk, new)
            if chunk < len(mixes):
                step = self.mix_last if chunk == task[0] else self.mix
                state = step(state, peak, chunk, old, task[0])
        if following is not None:
            self.top[...] = top
        if task is not None:
            task[2](peak, jnp.sum(state[0], axis=0, keepdims=True), state[1])


def kept_at(group, chunk):
    if isinstance(group, int):
        return group * (group + 1) // 2 + chunk
    return lax.div(group * (group + 1), 2) + chunk


def columns(group):
    if isinstance(group, int):
        return slice(group * QB, (group + 1) * QB)
    return pl.ds(pl.multiple_of(group * QB, QB), QB)


def student_forward(half, sq, sk, svt, ctx_t, scale, kept, work):
    score, top = work
    flash = Flash(half, sk, svt, top, kept)

    def task(group):
        at = columns(group)

        def finish(peak, total, acc):
            ctx_t[:, at] = acc / total
            scale[:, at] = jnp.broadcast_to(1.0 / total, (8, QB))

        return group, lambda: sq[at, :], finish

    tasks = [task(group) for group in (3, 2, 1, 0)]
    flash.step(None, None, tasks[0], score[0])
    for k in range(4):
        following = tasks[k + 1] if k < 3 else None
        flash.step(tasks[k], score[k % 2], following, score[(k + 1) % 2])


def teacher_forward(half, tq, tk, tvt, tctx_t, work, ready):
    score, top = work
    flash = Flash(half, tk, tvt, top)

    def task(head, group):
        at = columns(group)

        def finish(peak, total, acc):
            row = pl.multiple_of(head * D, D)
            tctx_t[pl.ds(row, D), at] = (acc / total).astype(BF16)

        return group, lambda: tq[head, at, :], finish

    ready(0)
    flash.step(None, None, task(0, 3), score[0])

    def pair(i, _):
        tasks = [task(2 * i, group) for group in (3, 2, 1, 0)]
        tasks += [task(2 * i + 1, group) for group in (0, 1, 2, 3)]
        for k in range(7):
            if k == 3:
                ready(2 * i + 1)
            flash.step(tasks[k], score[k % 2], tasks[k + 1], score[(k + 1) % 2])

        @pl.when(i == 0)
        def _():
            ready(2)
            flash.step(tasks[7], score[1], task(2, 3), score[0])

        @pl.when(i == 1)
        def _():
            flash.step(tasks[7], score[1], None, None)

        return 0

    lax.fori_loop(0, 2, pair, 0)


def turn_values(values, values_t):
    def chunk(i, _):
        values_t[i] = jnp.transpose(values[pl.ds(pl.multiple_of(i * KC, KC), KC), :])
        return 0

    lax.fori_loop(0, TOK // KC, chunk, 0)


def mismatches(tctx_t, proj_t, ctx_t, scale, grad_t, delta, loss):

    def step(group, _):
        at = columns(group)
        target = dot_nn(proj_t[...], tctx_t[:, at]).astype(BF16).astype(F32)
        context = ctx_t[:, at]
        miss = context - target
        per_total = scale[0:1, at]
        grad_t[:, at] = (miss * per_total).astype(BF16)
        dots = jnp.sum(fold(miss * context, jnp.add), axis=0, keepdims=True)
        delta[:, at] = jnp.broadcast_to(dots * per_total, (8, QB))
        squares = jnp.sum(fold(miss * miss, jnp.add), axis=0, keepdims=True) * (1.0 / 2048.0)
        wide = jnp.broadcast_to(squares, (8, QB))
        for i in range(4):
            loss[group * 4 + i] = wide[:, i * 128 : (i + 1) * 128]
        return 0

    lax.fori_loop(0, HALF // QB, step, 0)


def backward(first, sk_t, sv, grad_t, kept, delta, q_t, dq_t, dk, dv, dkv, dq, middle, after, send_dq, spin):
    dq_t[...] = jnp.zeros(dq_t.shape, F32)

    def outer(step, _):
        jb = lax.rem(first + step, TOK // KC)
        start = pl.multiple_of(jb * KC, KC)
        spans = [pl.ds(pl.multiple_of(start + e * 512, 512), 512) for e in range(2)]
        dk[...] = jnp.zeros(dk.shape, F32)
        dv[...] = jnp.zeros(dv.shape, F32)

        def terms(e, group, late=False):
            at, rows = columns(group), slice(e * 512, (e + 1) * 512)
            weights = kept.at[kept_at(group, jb)]
            if late:
                at = pl.ds(pl.multiple_of(group * QB + 256, 256), 256)
                prob = weights[rows, 256:]
            else:
                prob = weights[rows, :]
            query_t, grad = q_t[:, at], grad_t[:, at]
            ds = prob.astype(F32) * (dot_nn(sv[spans[e], :], grad) - delta[0:1, at])
            ds = ds.astype(BF16)
            dv[:, rows] += dot_nt(grad, prob)
            dk[:, rows] += dot_nt(query_t, ds)
            dq_t[:, at] += dot_nn(sk_t[jb, :, rows], ds)

        terms(0, jb)
        terms(1, jb, True)

        def leave(group):
            at = columns(group)
            dq[at, :] = (jnp.transpose(dq_t[:, at]) * ROOT).astype(BF16)
            send_dq(group)

        middle(step)

        @pl.when(jnp.logical_or(step + first >= TOK // KC, jnp.logical_and(first == 0, step >= 0)))
        def _():
            leave(jb)

        left = HALF // QB - 1 - jb

        def full(turn, _):
            group = jb + 1 + lax.rem(turn + spin, left)
            terms(0, group)
            terms(1, group)

            @pl.when(jnp.logical_and(step == TOK // KC - 1, first > 0))
            def _():
                leave(group)

            return 0

        lax.fori_loop(0, left, full, 0)
        for i in range(KC // 128):
            span = slice(i * 128, (i + 1) * 128)
            dkv[jb * 4 + i // 2, i % 2, :D, :] = (dk[:, span] * ROOT).astype(BF16)
            dkv[jb * 4 + i // 2, i % 2, D:, :] = dv[:, span].astype(BF16)
        after(step, jb)
        return 0

    lax.fori_loop(0, TOK // KC, outer, 0)


class Place:
    def __init__(self):
        self.section = lax.axis_index("section")
        self.s = lax.axis_index("seq")
        self.c = lax.rem(self.section, 2)
        self.base = self.section - self.c
        self.half = lax.rem(self.s, 2)
        self.h8 = head_of(self.s)
        self.head = self.c * 8 + self.h8
        self.me = self.c * NS + self.s


def head_of(s):
    return lax.rem(lax.div(s, 2), 4) * 2 + lax.div(s, 8)


def push(here, src, dst, send, recv, c, s):
    same = jnp.logical_and(c == here.c, s == here.s)

    @pl.when(same)
    def _():
        pltpu.make_async_copy(src, dst, recv).start()

    @pl.when(jnp.logical_not(same))
    def _():
        pltpu.make_async_remote_copy(
            src_ref=src, dst_ref=dst, send_sem=send, recv_sem=recv,
            device_id={"section": here.base + c, "seq": s}, device_id_type=MESH,
        ).start()


def toward(here, tx, tz):
    at = lax.div(here.s, 2)
    x = lax.rem(lax.div(at, 4) + tx, 2)
    z = lax.rem(lax.rem(at, 4) + jnp.where(here.half == 0, tz, 4 - tz), 4)
    return x * 4 + z


def greet(here):
    barrier = pltpu.get_barrier_semaphore()

    def signal(t, _):
        other = lax.rem(here.me + t, 2 * NS)
        pl.semaphore_signal(
            barrier, inc=1,
            device_id={"section": here.base + lax.div(other, NS), "seq": lax.rem(other, NS)},
            device_id_type=MESH,
        )
        return 0

    lax.fori_loop(1, 2 * NS, signal, 0)
    pl.semaphore_wait(barrier, 2 * NS - 1)


def drain(ref, sem):
    pltpu.make_async_copy(ref, ref, sem).wait()


S_K, S_V, S_Q, T_K, T_V, T_Q, G_Q, G_KV, LOSS = 0, 1, 2, 3, 4, 5, 9, 10, 11
FWD = 12
PAIR = 16
N_SEM = 20


def send_student(here, sq, sk, sv, sqb, skb, svb, send, recv):
    def step(t, _):
        c, p = lax.rem(here.c + lax.rem(t, 2), 2), toward(here, lax.rem(lax.div(t, 2), 2), lax.div(t, 4))
        h8 = head_of(2 * p)
        kv = pl.multiple_of((2 * c + lax.div(h8, 4)) * D, D)
        q = pl.multiple_of((c * 8 + h8) * D, D)
        at = pl.multiple_of(here.s * 256 + here.c * 128, 128)
        push(here, sk.at[0, :, pl.ds(kv, D)], skb.at[pl.ds(at, 128), :],
             send.at[S_K], recv.at[S_K], c, 2 * p)
        push(here, sv.at[0, :, pl.ds(kv, D)], svb.at[pl.ds(at, 128), :],
             send.at[S_V], recv.at[S_V], c, 2 * p + 1)
        to = pl.multiple_of(here.s * 128, 128)
        push(here, sq.at[0, :, pl.ds(q, D)], sqb.at[pl.ds(to, 128), :],
             send.at[S_Q], recv.at[S_Q], c, 2 * p + here.c)
        return 0

    lax.fori_loop(0, 16, step, 0)


def send_teacher(here, tq, tk, tv, tqb, tkb, tvb, send, recv):
    def step(t, _):
        p = toward(here, lax.rem(t, 2), lax.div(t, 2))
        kv = pl.multiple_of(lax.div(head_of(2 * p), 2) * D, D)
        at = pl.multiple_of(here.s * 256, 256)
        push(here, tk.at[0, :, pl.ds(kv, D)], tkb.at[pl.ds(at, 256), :],
             send.at[T_K], recv.at[T_K], here.c, 2 * p)
        push(here, tv.at[0, :, pl.ds(kv, D)], tvb.at[pl.ds(at, 256), :],
             send.at[T_V], recv.at[T_V], here.c, 2 * p + 1)
        return 0

    lax.fori_loop(0, 8, step, 0)
    for h in range(4):
        def query(t, _):
            p = toward(here, lax.rem(t, 2), lax.div(t, 2))
            col = pl.multiple_of(head_of(2 * p) * 512 + h * D, D)
            for core in range(2):
                push(here, tq.at[0, pl.ds(core * 128, 128), pl.ds(col, D)],
                     tqb.at[h, pl.ds(pl.multiple_of(here.s * 128, 128), 128), :],
                     send.at[T_Q + h], recv.at[T_Q + h], here.c, 2 * p + core)
            return 0

        lax.fori_loop(0, 8, query, 0)


def sibling(here, src, dst, send, recv):
    return pltpu.make_async_remote_copy(
        src_ref=src, dst_ref=dst, send_sem=send, recv_sem=recv,
        device_id={"section": here.section, "seq": here.s + 1 - 2 * here.half},
        device_id_type=MESH,
    )


def share(here, kb, vb, send, recv, k, v, fk, fv):
    @pl.when(here.half == 0)
    def _():
        drain(kb, recv.at[k])
        sibling(here, kb, kb, send.at[fk], recv.at[fk]).start()
        drain(vb, recv.at[fv])

    @pl.when(here.half == 1)
    def _():
        drain(vb, recv.at[v])
        sibling(here, vb, vb, send.at[fv], recv.at[fv]).start()
        drain(kb, recv.at[fk])


def kernel(tq, tk, tv, proj, sq, sk, sv, out_q, out_k, out_v, out_loss,
           tqb, tkb, tvb, tvt, sqb, skb, svb, svt, projb, ctx_t, scale, tctx_t, grad_t, delta, loss,
           kept, proj_t, q_t, dq_t, dk, dv, dkv, paired, summed, dq, got_kv, got_loss,
           score0, score1, top, send, recv, local):
    here = Place()
    work = ((score0, score1), top)
    own_proj = pltpu.make_async_copy(proj.at[0, here.h8], projb, local)
    own_proj.start()
    greet(here)
    send_student(here, sq, sk, sv, sqb, skb, svb, send, recv)
    send_teacher(here, tq, tk, tv, tqb, tkb, tvb, send, recv)
    share(here, skb, svb, send, recv, S_K, S_V, FWD, FWD + 1)
    turn_values(svb, svt)
    drain(sqb, recv.at[S_Q])
    q_t[...] = jnp.transpose(sqb[...])
    student_forward(here.half, sqb, skb, svt, ctx_t, scale, kept, work)
    turn_values(skb, svt)
    own_proj.wait()
    proj_t[...] = jnp.transpose(projb[...])
    share(here, tkb, tvb, send, recv, T_K, T_V, FWD + 2, FWD + 3)
    turn_values(tvb, tvt)

    def ready(head):
        drain(tqb.at[head], recv.at[T_Q + head])

    teacher_forward(here.half, tqb, tkb, tvt, tctx_t, work, ready)
    mismatches(tctx_t, proj_t, ctx_t, scale, grad_t, delta, loss)

    def send_loss(t, _):
        s = lax.rem(here.s + t, NS)
        push(here, loss.at[s], got_loss.at[here.head], send.at[LOSS], recv.at[LOSS], here.half, s)
        return 0

    z = lax.rem(lax.div(here.s, 2), 4)
    first = lax.rem(z + lax.div(here.s, 8) + 2 * here.c, 4)

    def finish_kv(step):
        jb = lax.rem(first + step, 4)
        drain(paired.at[step], recv.at[PAIR + step])

        def one(i, _):
            s = jb * 4 + i
            mine = dkv[s, here.half].astype(F32) + paired[step, i].astype(F32)
            summed[s] = mine.astype(BF16)
            push(here, summed.at[s], got_kv.at[here.head], send.at[G_KV], recv.at[G_KV],
                 here.half, s)
            return 0

        lax.fori_loop(0, 4, one, 0)

    def after(step, jb):
        sibling(here, dkv.at[pl.ds(jb * 4, 4), 1 - here.half], paired.at[step],
                send.at[PAIR], recv.at[PAIR + step]).start()

    def middle(step):
        @pl.when(step > 0)
        def _():
            finish_kv(step - 1)

        @pl.when(step == 1)
        def _():
            lax.fori_loop(0, NS, send_loss, 0)

    def send_dq(group):
        def one(i, _):
            s = group * 4 + i
            row = pl.multiple_of(s * 128, 128)
            col = pl.multiple_of(here.head * D, D)
            push(here, dq.at[pl.ds(row, 128), :], out_q.at[0, :, pl.ds(col, D)],
                 send.at[G_Q], recv.at[G_Q], here.half, s)
            return 0

        lax.fori_loop(0, 4, one, 0)

    backward(first, svt, svb, grad_t, kept, delta, q_t, dq_t, dk, dv, dkv, dq,
             middle, after, send_dq, z)
    finish_kv(3)

    drain(got_loss, recv.at[LOSS])
    sums = got_loss[0]
    for h in range(1, 16):
        sums = sums + got_loss[h]
    out_loss[...] = sums[0:1, :]
    drain(got_kv, recv.at[G_KV])
    for g in range(4):
        sums = got_kv[g * 4].astype(F32)
        for i in range(1, 4):
            sums = sums + got_kv[g * 4 + i].astype(F32)
        out_k[0, :, g * D : (g + 1) * D] = jnp.transpose(sums[:D])
        out_v[0, :, g * D : (g + 1) * D] = jnp.transpose(sums[D:])
    drain(out_q, recv.at[G_Q])

    own_core = here.half == 0

    @pl.when(own_core)
    def _():
        drain(skb.at[pl.ds(0, 15 * 128), :], send.at[S_K])
        drain(svb.at[pl.ds(0, 16 * 128), :], send.at[S_V])
        drain(tkb.at[pl.ds(0, 7 * 256), :], send.at[T_K])
        drain(tvb.at[pl.ds(0, 8 * 256), :], send.at[T_V])
        drain(skb, send.at[FWD])
        drain(tkb, send.at[FWD + 2])

    @pl.when(jnp.logical_not(own_core))
    def _():
        drain(skb.at[pl.ds(0, 16 * 128), :], send.at[S_K])
        drain(svb.at[pl.ds(0, 15 * 128), :], send.at[S_V])
        drain(tkb.at[pl.ds(0, 8 * 256), :], send.at[T_K])
        drain(tvb.at[pl.ds(0, 7 * 256), :], send.at[T_V])
        drain(svb, send.at[FWD + 1])
        drain(tvb, send.at[FWD + 3])

    for h in range(4):
        drain(tqb.at[h, pl.ds(0, 15 * 128), :], send.at[T_Q + h])
    drain(paired, send.at[PAIR])
    with_self = here.half == here.c

    @pl.when(with_self)
    def _():
        drain(sqb.at[pl.ds(0, 15 * 128), :], send.at[S_Q])
        drain(dq.at[pl.ds(0, 15 * 128), :], send.at[G_Q])
        drain(loss.at[pl.ds(0, 15)], send.at[LOSS])
        drain(got_kv.at[pl.ds(0, 15)], send.at[G_KV])

    @pl.when(jnp.logical_not(with_self))
    def _():
        drain(sqb, send.at[S_Q])
        drain(dq, send.at[G_Q])
        drain(loss, send.at[LOSS])
        drain(got_kv, send.at[G_KV])


def body(tq, tk, tv, proj, sq, sk, sv):
    vmem = pltpu.VMEM
    dq, dk, dv, loss = pl.pallas_call(
        kernel,
        out_shape=(
            jax.ShapeDtypeStruct((1, 128, 2048), BF16),
            jax.ShapeDtypeStruct((1, 128, 512), F32),
            jax.ShapeDtypeStruct((1, 128, 512), F32),
            jax.ShapeDtypeStruct((1, 128), F32),
        ),
        in_specs=[pl.BlockSpec(memory_space=pl.ANY)] * 7,
        out_specs=(
            pl.BlockSpec(memory_space=pl.ANY),
            pl.BlockSpec(memory_space=vmem),
            pl.BlockSpec(memory_space=vmem),
            pl.BlockSpec(memory_space=vmem),
        ),
        scratch_shapes=[
            vmem((4, HALF, D), BF16),
            vmem((TOK, D), BF16),
            vmem((TOK, D), BF16),
            vmem((TOK // KC, D, KC), BF16),
            vmem((HALF, D), BF16),
            vmem((TOK, D), BF16),
            vmem((TOK, D), BF16),
            vmem((TOK // KC, D, KC), BF16),
            vmem((512, D), BF16),
            vmem((D, HALF), F32),
            vmem((8, HALF), F32),
            vmem((4 * D, HALF), BF16),
            vmem((D, HALF), BF16),
            vmem((8, HALF), F32),
            vmem((NS, 8, 128), F32),
            vmem((10, KC, QB), BF16),
            vmem((D, 512), BF16),
            vmem((D, HALF), BF16),
            vmem((D, HALF), F32),
            vmem((D, KC), F32),
            vmem((D, KC), F32),
            vmem((NS, 2, 2 * D, 128), BF16),
            vmem((4, 4, 2 * D, 128), BF16),
            vmem((NS, 2 * D, 128), BF16),
            vmem((HALF, D), BF16),
            vmem((NS, 2 * D, 128), BF16),
            vmem((NS, 8, 128), F32),
            vmem((TOK, QB), F32),
            vmem((TOK, QB), F32),
            vmem((8, QB), F32),
            pltpu.SemaphoreType.DMA((N_SEM,)),
            pltpu.SemaphoreType.DMA((N_SEM,)),
            pltpu.SemaphoreType.DMA,
        ],
        compiler_params=pltpu.CompilerParams(
            collective_id=0, has_side_effects=True, vmem_limit_bytes=60 * 1024 * 1024
        ),
        cost_estimate=pl.CostEstimate(
            flops=17_000_000_000, bytes_accessed=8_000_000, transcendentals=30_000_000
        ),
    )(tq, tk, tv, proj, sq, sk, sv)
    return dq.astype(F32), dk, dv, loss


def solution(mesh):
    rows = P("section", "seq", None)
    return jax.shard_map(
        body,
        mesh=mesh,
        in_specs=(rows, rows, rows, P("section", None, None, None), rows, rows, rows),
        out_specs=(rows, rows, rows, P("section", "seq")),
        check_vma=False,
    )
```
